32 devices in a mesh: dp: 16 (over z, y, x), sub: 2 (over core).
Axes of the slice: x: 2, y: 2, z: 4, core: 2. Of those that a mesh axis runs over, the one named last changes fastest.
Arguments:
- queries: bfloat16 [6144, 4096], P('dp', 'sub'), may hold values from -32 to 32
- passages: bfloat16 [6144, 4096], P('dp', 'sub'), may hold values from -8 to 8
- positive: int32 [16, 384], P('dp'), may hold values from 0 to 383, each once within a row
- pair_on: int32 [16, 3], replicated, may hold values from 0 to 1, as said below
Outputs:
- loss: float32 [1], replicated
- query_grad: float32 [6144, 4096], P('dp', 'sub')
- passage_grad: float32 [6144, 4096], P('dp', 'sub')
The draws below stay inside these ranges and needn't reach their ends.
Inputs may be any that keep to these rules, and one draw needn't show every extreme that they name: pair_on[s, k] equals pair_on[s xor 2 ** (log2(16) - 3 + k), k]; shards 0 and 2 ** (log2(16) - 3) - 1 pair at every level.
All inputs are finite; a program needn't handle non-finite values.
Results may differ from the reference program's by a relative error of at most 0.0016.
Values may be sent and summed in bfloat16 or wider, within the bound.
No kernel may reach another device: no remote copies, remote signals or barrier semaphores. Data moves between devices by JAX's collectives and lax.ppermute only.
A program may use at most 128 MiB of HBM per device.

```python
import math
import jax
import jax.numpy as jnp
from jax import lax

D = 4096
R = 384
PB = 3
TOTAL = 6144
N_DP = 16


def draw_queries(key, part):
    key = jax.random.fold_in(key, 1)
    values = jnp.clip(jax.random.normal(key, (TOTAL, D), jnp.float32), -6.0, 6.0)
    return values.astype(jnp.bfloat16)


def draw_passages(key, part):
    key = jax.random.fold_in(key, 2)
    values = jnp.clip(jax.random.normal(key, (TOTAL, D), jnp.float32), -6.0, 6.0)
    return values.astype(jnp.bfloat16)


def draw_pair_on(key, part):
    key = jax.random.fold_in(key, 3)
    depth = N_DP.bit_length() - 1
    coins = jax.random.randint(key, (N_DP, PB), 0, 2)
    coins = coins.at[0].set(1)
    coins = coins.at[(1 << depth - PB) - 1].set(1)
    shards = jnp.arange(N_DP, dtype=jnp.int32)[:, None]
    masks = jnp.array([1 << depth - PB + k for k in range(PB)], jnp.int32)[None, :]
    base_rows = jnp.bitwise_and(shards, jnp.bitwise_not(masks))
    levels = jnp.arange(PB, dtype=jnp.int32)[None, :]
    return coins[base_rows, levels].astype(jnp.int32)


def setup_inputs(seed: int = 0) -> dict:
    key_list = jax.random.split(jax.random.key(seed), 5)
    queries = draw_queries(jax.random.fold_in(key_list[4], 71), 0)
    passages = draw_passages(jax.random.fold_in(key_list[4], 71), 0)
    positive = jax.vmap(lambda own: jax.random.permutation(own, R))(jax.random.split(key_list[2], N_DP)).reshape((N_DP, R)).astype(jnp.int32)
    pair_on = draw_pair_on(jax.random.fold_in(key_list[4], 71), 0)
    return dict(queries=queries, passages=passages, positive=positive, pair_on=pair_on)


def tile_logits(left, right):
    return lax.dot_general(left, right, (((1,), (1,)), ((), ())), preferred_element_type=jnp.float32) / math.sqrt(D)

def lse_axis(values, axis):
    return jax.scipy.special.logsumexp(values, axis=axis)

def reference(queries, passages, positive, pair_on):
    depth = N_DP.bit_length() - 1
    query_blocks = queries.reshape(N_DP, R, D)
    passage_blocks = passages.reshape(N_DP, R, D)
    level_bits = jnp.array([1 << depth - PB + k for k in range(PB)], jnp.int32)
    columns = jnp.arange(R, dtype=jnp.int32)

    def first_pass(shard):
        mine_q = query_blocks[shard]
        mine_p = passage_blocks[shard]
        own = tile_logits(mine_q, mine_p)
        row = lse_axis(own, 1)
        col = lse_axis(own, 0)
        for k in range(PB):
            other = jnp.bitwise_xor(shard, level_bits[k])
            active = pair_on[shard, k] > 0
            upper = tile_logits(mine_q, passage_blocks[other])
            lower = tile_logits(query_blocks[other], mine_p)
            row = jnp.where(active, jnp.logaddexp(row, lse_axis(upper, 1)), row)
            col = jnp.where(active, jnp.logaddexp(col, lse_axis(lower, 0)), col)
        onehot = (positive[shard][:, None] == columns[None, :]).astype(jnp.float32)
        return (row, col, jnp.sum(own * onehot))
    rows_lse, cols_lse, pos_sums = lax.map(first_pass, jnp.arange(N_DP, dtype=jnp.int32))

    def second_pass(shard):
        mine_q = query_blocks[shard]
        mine_p = passage_blocks[shard]
        own = tile_logits(mine_q, mine_p)
        onehot = (positive[shard][:, None] == columns[None, :]).astype(jnp.float32)
        grad = (jnp.exp(own - rows_lse[shard][:, None]) + jnp.exp(own - cols_lse[shard][None, :]) - 2.0 * onehot).astype(jnp.bfloat16)
        dq = jnp.dot(grad, mine_p, preferred_element_type=jnp.float32)
        dp = lax.dot_general(grad, mine_q, (((0,), (0,)), ((), ())), preferred_element_type=jnp.float32)
        for k in range(PB):
            other = jnp.bitwise_xor(shard, level_bits[k])
            active = pair_on[shard, k] > 0
            far_q = query_blocks[other]
            far_p = passage_blocks[other]
            upper = tile_logits(mine_q, far_p)
            lower = tile_logits(far_q, mine_p)
            g_up = jnp.exp(upper - rows_lse[shard][:, None]) + jnp.exp(upper - cols_lse[other][None, :])
            g_low = jnp.exp(lower - rows_lse[other][:, None]) + jnp.exp(lower - cols_lse[shard][None, :])
            g_up = jnp.where(active, g_up, 0.0).astype(jnp.bfloat16)
            g_low = jnp.where(active, g_low, 0.0).astype(jnp.bfloat16)
            dq = dq + jnp.dot(g_up, far_p, preferred_element_type=jnp.float32)
            dp = dp + lax.dot_general(g_low, far_q, (((0,), (0,)), ((), ())), preferred_element_type=jnp.float32)
        return (dq, dp)
    dq_all, dp_all = lax.map(second_pass, jnp.arange(N_DP, dtype=jnp.int32))
    total = jnp.sum(rows_lse) + jnp.sum(cols_lse) - 2.0 * jnp.sum(pos_sums)
    loss = jnp.reshape(total / (2.0 * TOTAL), (1,))
    return (loss, dq_all.reshape(TOTAL, D), dp_all.reshape(TOTAL, D))
```

```python
import functools
import math

import jax
import jax.numpy as jnp
from jax import lax
from jax.experimental import pallas as pl
from jax.experimental.pallas import tpu as pltpu
from jax.sharding import PartitionSpec as P

D = 4096
ABSENT = -1e30


def exchanged(block, axis, offset):
    count = lax.axis_size(axis)
    return lax.ppermute(block, axis, [(i, i ^ offset) for i in range(count)])


def call(kernel, out_shape, operands, **kwargs):
    scalars, unread = kwargs.pop("scalars", 0), kwargs.pop("unread", 0)
    flops = kwargs.pop("flops", 0)
    kwargs["in_specs"] = (
        [pl.BlockSpec(memory_space=pltpu.SMEM)] * scalars
        + [pl.BlockSpec(memory_space=pltpu.VMEM)] * (len(operands) - scalars - unread)
        + [pl.BlockSpec(memory_space=pl.ANY)] * unread
    )
    if "out_specs" not in kwargs:
        kwargs["out_specs"] = jax.tree.map(
            lambda _: pl.BlockSpec(memory_space=pltpu.VMEM), out_shape
        )
    return pl.pallas_call(
        kernel,
        out_shape=out_shape,
        compiler_params=pltpu.CompilerParams(vmem_limit_bytes=20 * 1024 * 1024),
        cost_estimate=pl.CostEstimate(flops=flops, bytes_accessed=0, transcendentals=0),
        **kwargs,
    )(*operands)


def f32(*shape):
    return jax.ShapeDtypeStruct(shape, jnp.float32)


def bf16(*shape):
    return jax.ShapeDtypeStruct(shape, jnp.bfloat16)


def rows_kernel(count, right_ref, *refs):
    for ref, out_ref in zip(refs[:count], refs[-count:]):
        out_ref[...] = lax.dot_general(
            ref[...],
            right_ref[...],
            (((1,), (1,)), ((), ())),
            preferred_element_type=jnp.float32,
        )


def partial_rows(right, blocks, after=()):
    return call(
        functools.partial(rows_kernel, len(blocks)),
        [f32(block.shape[0], right.shape[0]) for block in blocks],
        [right, *blocks, *after],
        unread=len(after),
    )


def tiles_kernel(count, left_ref, *refs):
    out_ref = refs[-1]
    for k, ref in enumerate(refs[:count]):
        out_ref[k] = lax.dot_general(
            left_ref[...],
            ref[...],
            (((1,), (1,)), ((), ())),
            preferred_element_type=jnp.float32,
        )


def partial_tiles(left, blocks, after=()):
    rows, count = left.shape[0], len(blocks)
    return call(
        functools.partial(tiles_kernel, count),
        f32(count, rows, rows),
        [left, *blocks, *after],
        unread=len(after),
    )


def copy_kernel(first, array_ref, *refs):
    refs[-1][...] = array_ref[first : first + refs[-1].shape[0], :]


def rows_after(array, first, count, earlier):
    return call(
        functools.partial(copy_kernel, first),
        jax.ShapeDtypeStruct((count, array.shape[1]), array.dtype),
        [array, *earlier],
        unread=len(earlier),
    )


def pass_kernel(*refs):
    pass


def held_until(array, earlier):
    count = 1 + len(earlier)
    return pl.pallas_call(
        pass_kernel,
        out_shape=jax.ShapeDtypeStruct(array.shape, array.dtype),
        in_specs=[pl.BlockSpec(memory_space=pl.ANY)] * count,
        out_specs=pl.BlockSpec(memory_space=pl.ANY),
        input_output_aliases={0: 0},
        cost_estimate=pl.CostEstimate(flops=0, bytes_accessed=0, transcendentals=0),
    )(array, *earlier)


def join_kernel(upper_ref, lower_ref, out_ref):
    out_ref[: upper_ref.shape[0], :] = upper_ref[...]
    out_ref[upper_ref.shape[0] :, :] = lower_ref[...]


def joined(upper, lower):
    shape = (upper.shape[0] + lower.shape[0], upper.shape[1])
    return call(join_kernel, jax.ShapeDtypeStruct(shape, upper.dtype), [upper, lower])


def stack_kernel(count, *refs):
    for k in range(count):
        refs[-1][k] = refs[k][...]


def as_row(column, rows):
    i = lax.broadcasted_iota(jnp.int32, (rows, rows), 0)
    j = lax.broadcasted_iota(jnp.int32, (rows, rows), 1)
    return jnp.sum(jnp.where(i == j, column, 0.0), axis=0, keepdims=True)


def as_column(row, rows):
    i = lax.broadcasted_iota(jnp.int32, (rows, rows), 0)
    j = lax.broadcasted_iota(jnp.int32, (rows, rows), 1)
    return jnp.sum(jnp.where(i == j, row, 0.0), axis=1, keepdims=True)


def stats_kernel(levels, slots, unread, act_ref, *refs):
    *refs, tile_ref, row_ref, pack_ref = refs
    *part_refs, pos_ref = refs[: len(refs) - unread]
    rows = tile_ref.shape[1]
    scale = 1.0 / math.sqrt(D)
    slots = iter(slots)
    for mine_ref, other_ref in zip(part_refs[0::2], part_refs[1::2]):
        for k in range(mine_ref.shape[0]):
            tile_ref[next(slots)] = (mine_ref[k] + other_ref[k]) * scale
    top = jnp.max(tile_ref[0], axis=1, keepdims=True)
    for k in range(levels):
        seen = jnp.max(tile_ref[k + 1], axis=1, keepdims=True)
        top = jnp.where(act_ref[k] > 0, jnp.maximum(top, seen), top)
    total = jnp.sum(jnp.exp(tile_ref[0] - top), axis=1, keepdims=True)
    for k in range(levels):
        seen = jnp.sum(jnp.exp(tile_ref[k + 1] - top), axis=1, keepdims=True)
        total = jnp.where(act_ref[k] > 0, total + seen, total)
    row_lse = top + jnp.log(total)
    row_ref[...] = row_lse
    pack_ref[...] = jnp.zeros_like(pack_ref)
    for k in range(levels + 1):
        tile = tile_ref[k]
        high = jnp.max(tile, axis=0, keepdims=True)
        col = high + jnp.log(jnp.sum(jnp.exp(tile - high), axis=0, keepdims=True))
        if k == 0:
            pack_ref[levels : levels + 1, :] = col
        else:
            pack_ref[k - 1 : k, :] = jnp.where(act_ref[k - 1] > 0, col, ABSENT)
    pack_ref[levels + 1 : levels + 2, :] = as_row(row_lse, rows)
    columns = lax.broadcasted_iota(jnp.int32, (rows, rows), 1)
    picked = jnp.where(pos_ref[...] == columns, tile_ref[0], 0.0)
    picked = jnp.sum(jnp.sum(picked, axis=1, keepdims=True), axis=0, keepdims=True)
    pack_ref[levels + 2 : levels + 3, :] = jnp.broadcast_to(picked, (1, rows))


def grads_kernel(
    levels, act_ref, tile_ref, row_ref, pos_ref, *refs
):
    group = 1 << levels
    packs = refs[:group]
    grad_ref, back_ref, col_ref, far_ref, loss_ref = refs[group:]
    rows = tile_ref.shape[1]

    def columns_of(member):
        terms = [packs[member][levels : levels + 1, :]]
        for k in range(levels):
            terms.append(packs[member ^ 1 << k][k : k + 1, :])
        top = functools.reduce(jnp.maximum, terms)
        return top + jnp.log(sum(jnp.exp(term - top) for term in terms))

    col_lses = [columns_of(member) for member in range(group)]
    loss = jnp.zeros((1, 1), jnp.float32)
    for member in range(group):
        line = col_lses[member] + packs[member][levels + 1 : levels + 2, :]
        loss += jnp.sum(line, axis=1, keepdims=True)
        loss -= 2.0 * packs[member][levels + 2 : levels + 3, 0:1]
    loss_ref[...] = jnp.broadcast_to(loss, loss_ref.shape)

    far_ref[...] = jnp.zeros_like(far_ref)
    col_ref[...] = jnp.zeros_like(col_ref)
    for k in range(levels):
        far = packs[1 << k][levels + 1 : levels + 2, :]
        far = jnp.where(act_ref[k] > 0, far, -ABSENT)
        far_ref[:, k : k + 1] = as_column(far, rows)
        col_ref[k : k + 1, :] = jnp.where(act_ref[k] > 0, col_lses[0], -ABSENT)
    row_lse = row_ref[...]
    own = tile_ref[0]
    columns = lax.broadcasted_iota(jnp.int32, (rows, rows), 1)
    onehot = jnp.where(pos_ref[...] == columns, 2.0, 0.0)
    grad = jnp.exp(own - row_lse) + jnp.exp(own - col_lses[0]) - onehot
    grad_ref[0] = grad.astype(jnp.bfloat16)
    back_ref[...] = grad.T.astype(jnp.bfloat16)
    for k in range(levels):
        tile = tile_ref[k + 1]
        grad = jnp.exp(tile - row_lse) + jnp.exp(tile - col_lses[1 << k])
        grad_ref[k + 1] = jnp.where(act_ref[k] > 0, grad, 0.0).astype(jnp.bfloat16)


def dot(left, right):
    return jnp.dot(left, right, preferred_element_type=jnp.float32)


STEP = 512


def column_blocks(width):
    return [slice(first, first + STEP) for first in range(0, width, STEP)]


def copied_out(buffer_ref, out_ref, sems, j, cols):
    return pltpu.make_async_copy(buffer_ref.at[j], out_ref.at[:, cols], sems.at[j])


def copy_scratch(rows, width):
    steps = width // STEP
    return [pltpu.VMEM((steps, rows, STEP), jnp.float32), pltpu.SemaphoreType.DMA((steps,))]


def query_kernel(count, grad_ref, *refs):
    out_ref, token_ref, buffer_ref, sems = refs[count:]
    token_ref[...] = jnp.zeros_like(token_ref)
    blocks = column_blocks(out_ref.shape[1])
    for j, cols in enumerate(blocks):
        total = dot(grad_ref[0], refs[0][:, cols])
        for k in range(1, count):
            total += dot(grad_ref[k], refs[k][:, cols])
        buffer_ref[j] = total
        copied_out(buffer_ref, out_ref, sems, j, cols).start()
    for j, cols in enumerate(blocks):
        copied_out(buffer_ref, out_ref, sems, j, cols).wait()


def query_product(grads, blocks):
    count, rows, width = len(blocks), *blocks[0].shape
    return call(
        functools.partial(query_kernel, count),
        (f32(rows, width), f32(8, 128)),
        [grads, *blocks],
        out_specs=(
            pl.BlockSpec(memory_space=pl.ANY),
            pl.BlockSpec(memory_space=pltpu.VMEM),
        ),
        scratch_shapes=copy_scratch(rows, width),
    )


def passage_kernel(pieces, last, col_ref, far_ref, *refs):
    count = len(pieces)
    parts, refs = refs[: 2 * count], refs[2 * count :]
    heads = 1 if last else 2
    head, blocks = refs[:heads], refs[heads : heads + count]
    out_ref, *scratch = refs[heads + count :]
    grads = scratch[:count]
    for n, (k, start) in enumerate(pieces):
        rows = blocks[n].shape[0]
        tile = (parts[2 * n][...] + parts[2 * n + 1][...]) * (1.0 / math.sqrt(D))
        far = far_ref[start : start + rows, k : k + 1]
        grad = jnp.exp(tile - far) + jnp.exp(tile - col_ref[k : k + 1, :])
        grads[n][...] = grad.T.astype(jnp.bfloat16)

    columns = column_blocks(out_ref.shape[1])
    for j, cols in enumerate(columns):
        if last:
            total = head[0][:, cols]
        else:
            total = dot(head[0][...], head[1][:, cols])
        for grad_ref, block in zip(grads, blocks):
            total += dot(grad_ref[...], block[:, cols])
        if last:
            buffer_ref, sems = scratch[count:]
            buffer_ref[j] = total
            copied_out(buffer_ref, out_ref, sems, j, cols).start()
        else:
            out_ref[:, cols] = total
    if last:
        for j, cols in enumerate(columns):
            copied_out(buffer_ref, out_ref, sems, j, cols).wait()


def passage_product(col, far, head, parts, pieces, blocks, last):
    rows, width = far.shape[0], blocks[0].shape[1]
    scratch = [pltpu.VMEM((rows, block.shape[0]), jnp.bfloat16) for block in blocks]
    if last:
        scratch += copy_scratch(rows, width)
    return call(
        functools.partial(passage_kernel, pieces, last),
        f32(rows, width),
        [col, far, *parts, *head, *blocks],
        out_specs=pl.BlockSpec(memory_space=pl.ANY if last else pltpu.VMEM),
        scratch_shapes=scratch,
    )


def local(queries, passages, positive, pair_on):
    rows, _ = queries.shape
    levels = pair_on.shape[1]
    me = lax.axis_index("dp")
    shards = lax.axis_size("dp")
    low = shards.bit_length() - 1 - levels
    masks = [1 << low + k for k in range(levels)]
    active = pair_on[me]
    place = positive.reshape(rows, 1)

    first = rows // 2
    upper = list(reversed(range(1, levels)))
    far_p = [None] * levels
    for k in reversed(range(levels)):
        far_p[k] = exchanged(passages, "dp", masks[k])
    part = 5 * rows // 6
    far_upper = exchanged(queries[:part], "dp", masks[0])
    far_q = joined(far_upper, exchanged(queries[part:], "dp", masks[0]))
    head = held_until(rows_after(queries, 0, first, []), [far_upper])
    heads = [exchanged(head, "dp", masks[k]) for k in upper]

    early = partial_tiles(queries, [passages, far_p[0]])
    early_other = exchanged(early, "sub", 1)
    late = [
        partial_tiles(queries, [block], [early_other])
        for block in [far_p[k] for k in upper]
    ]
    late_parts = []
    for part in late:
        late_parts += [part, exchanged(part, "sub", 1)]
    (near,) = partial_rows(passages, [far_q])
    near = [near, exchanged(near, "sub", 1)]
    tiles, row_lse, pack = call(
        functools.partial(stats_kernel, levels, [0, 1] + [k + 1 for k in upper], 1),
        (f32(levels + 1, rows, rows), f32(rows, 1), f32(8, rows)),
        [
            active,
            early, early_other,
            *late_parts,
            place,
            near[1],
        ],
        scalars=1,
        unread=1,
    )

    group = 1 << levels
    packs = [None] * group
    packs[0] = pack
    for member in range(3, group, 2):
        offset = sum(masks[k] for k in range(levels) if member >> k & 1)
        packs[member] = exchanged(pack, "dp", offset)
    come = [packs[member | (member > 1)] for member in range(0, group, 2)]
    tails = [
        exchanged(rows_after(queries, first, rows - first, [pack, piece]), "dp", masks[k])
        for k, piece in zip(upper, heads)
    ]
    bundle = call(
        functools.partial(stack_kernel, len(come)),
        f32(len(come), *pack.shape),
        come,
    )
    swapped = exchanged(bundle, "dp", masks[0])
    for n in range(group // 2):
        packs[2 * n if n else 1] = swapped[n]

    grads, back, col_lse, far_lse, total = call(
        functools.partial(grads_kernel, levels),
        (
            bf16(levels + 1, rows, rows),
            bf16(rows, rows),
            f32(8, rows),
            f32(rows, 8),
            f32(8, 128),
        ),
        [active, tiles, row_lse, place, *packs],
        scalars=1,
        flops=5405000000,
    )
    total = total[0, :1]
    for bit in range(low):
        total = total + exchanged(total, "dp", 1 << bit)
    loss = total / (2.0 * rows * shards)

    query_grad, token = query_product(grads, [passages, *far_p])

    parts = near
    for part in partial_rows(passages, heads, [bundle]):
        parts += [part, exchanged(part, "sub", 1)]
    passage_grad = passage_product(
        col_lse,
        far_lse,
        [back, queries],
        parts,
        [(0, 0)] + [(k, 0) for k in upper],
        [far_q, *heads],
        last=False,
    )
    ends = []
    for tail in tails:
        (part,) = partial_rows(passages, [tail], ends[-2:-1] or [token, passage_grad, loss])
        ends += [part, exchanged(part, "sub", 1)]
    passage_grad = passage_product(
        col_lse,
        far_lse,
        [passage_grad],
        ends,
        [(k, first) for k in upper],
        tails,
        last=True,
    )
    return (loss, query_grad, passage_grad)


def solution(mesh):
    placed = (P("dp", "sub"), P("dp", "sub"), P("dp", None), P())
    return jax.shard_map(
        local,
        mesh=mesh,
        in_specs=placed,
        out_specs=(P(), P("dp", "sub"), P("dp", "sub")),
        check_vma=False,
    )
```

```python
import functools
import math

import jax
import jax.numpy as jnp
from jax import lax
from jax.experimental import pallas as pl
from jax.experimental.pallas import tpu as pltpu
from jax.sharding import PartitionSpec as P

D = 4096
ABSENT = -1e30


def exchanged(block, axis, offset):
    count = lax.axis_size(axis)
    return lax.ppermute(block, axis, [(i, i ^ offset) for i in range(count)])


def call(kernel, out_shape, operands, **kwargs):
    scalars, unread = kwargs.pop("scalars", 0), kwargs.pop("unread", 0)
    flops = kwargs.pop("flops", 0)
    kwargs["in_specs"] = (
        [pl.BlockSpec(memory_space=pltpu.SMEM)] * scalars
        + [pl.BlockSpec(memory_space=pltpu.VMEM)] * (len(operands) - scalars - unread)
        + [pl.BlockSpec(memory_space=pl.ANY)] * unread
    )
    if "out_specs" not in kwargs:
        kwargs["out_specs"] = jax.tree.map(
            lambda _: pl.BlockSpec(memory_space=pltpu.VMEM), out_shape
        )
    return pl.pallas_call(
        kernel,
        out_shape=out_shape,
        compiler_params=pltpu.CompilerParams(vmem_limit_bytes=12 * 1024 * 1024),
        cost_estimate=pl.CostEstimate(flops=flops, bytes_accessed=0, transcendentals=0),
        **kwargs,
    )(*operands)


def f32(*shape):
    return jax.ShapeDtypeStruct(shape, jnp.float32)


def bf16(*shape):
    return jax.ShapeDtypeStruct(shape, jnp.bfloat16)


def rows_kernel(count, right_ref, *refs):
    for ref, out_ref in zip(refs[:count], refs[-count:]):
        out_ref[...] = lax.dot_general(
            ref[...],
            right_ref[...],
            (((1,), (1,)), ((), ())),
            preferred_element_type=jnp.float32,
        )


def partial_rows(right, blocks, after=()):
    return call(
        functools.partial(rows_kernel, len(blocks)),
        [f32(block.shape[0], right.shape[0]) for block in blocks],
        [right, *blocks, *after],
        unread=len(after),
    )


def stacked_rows_kernel(count, right_ref, *refs):
    for n in range(count):
        refs[-1][n] = lax.dot_general(
            refs[n][...],
            right_ref[...],
            (((1,), (1,)), ((), ())),
            preferred_element_type=jnp.float32,
        )


def partial_stack(right, blocks, after):
    return call(
        functools.partial(stacked_rows_kernel, len(blocks)),
        f32(len(blocks), blocks[0].shape[0], right.shape[0]),
        [right, *blocks, *after],
        unread=len(after),
    )


def tiles_kernel(count, left_ref, *refs):
    out_ref = refs[-1]
    for k, ref in enumerate(refs[:count]):
        out_ref[k] = lax.dot_general(
            left_ref[...],
            ref[...],
            (((1,), (1,)), ((), ())),
            preferred_element_type=jnp.float32,
        )


def partial_tiles(left, blocks, after=()):
    rows, count = left.shape[0], len(blocks)
    return call(
        functools.partial(tiles_kernel, count),
        f32(count, rows, rows),
        [left, *blocks, *after],
        unread=len(after),
    )


def copy_kernel(first, array_ref, *refs):
    refs[-1][...] = array_ref[first : first + refs[-1].shape[0], :]


def rows_after(array, first, count, earlier):
    return call(
        functools.partial(copy_kernel, first),
        jax.ShapeDtypeStruct((count, array.shape[1]), array.dtype),
        [array, *earlier],
        unread=len(earlier),
    )


def pass_kernel(*refs):
    pass


def held_until(array, earlier):
    count = 1 + len(earlier)
    return pl.pallas_call(
        pass_kernel,
        out_shape=jax.ShapeDtypeStruct(array.shape, array.dtype),
        in_specs=[pl.BlockSpec(memory_space=pl.ANY)] * count,
        out_specs=pl.BlockSpec(memory_space=pl.ANY),
        input_output_aliases={0: 0},
        cost_estimate=pl.CostEstimate(flops=0, bytes_accessed=0, transcendentals=0),
    )(array, *earlier)


def join_kernel(upper_ref, lower_ref, out_ref):
    out_ref[: upper_ref.shape[0], :] = upper_ref[...]
    out_ref[upper_ref.shape[0] :, :] = lower_ref[...]


def joined(upper, lower):
    shape = (upper.shape[0] + lower.shape[0], upper.shape[1])
    return call(join_kernel, jax.ShapeDtypeStruct(shape, upper.dtype), [upper, lower])


def stack_kernel(count, *refs):
    for k in range(count):
        refs[-1][k] = refs[k][...]


def as_row(column, rows):
    i = lax.broadcasted_iota(jnp.int32, (rows, rows), 0)
    j = lax.broadcasted_iota(jnp.int32, (rows, rows), 1)
    return jnp.sum(jnp.where(i == j, column, 0.0), axis=0, keepdims=True)


def as_column(row, rows):
    i = lax.broadcasted_iota(jnp.int32, (rows, rows), 0)
    j = lax.broadcasted_iota(jnp.int32, (rows, rows), 1)
    return jnp.sum(jnp.where(i == j, row, 0.0), axis=1, keepdims=True)


def stats_kernel(levels, slots, unread, act_ref, *refs):
    *refs, tile_ref, row_ref, pack_ref = refs
    *part_refs, pos_ref = refs[: len(refs) - unread]
    rows = tile_ref.shape[1]
    scale = 1.0 / math.sqrt(D)
    slots = iter(slots)
    for mine_ref, other_ref in zip(part_refs[0::2], part_refs[1::2]):
        for k in range(mine_ref.shape[0]):
            tile_ref[next(slots)] = (mine_ref[k] + other_ref[k]) * scale
    top = jnp.max(tile_ref[0], axis=1, keepdims=True)
    for k in range(levels):
        seen = jnp.max(tile_ref[k + 1], axis=1, keepdims=True)
        top = jnp.where(act_ref[k] > 0, jnp.maximum(top, seen), top)
    total = jnp.sum(jnp.exp(tile_ref[0] - top), axis=1, keepdims=True)
    for k in range(levels):
        seen = jnp.sum(jnp.exp(tile_ref[k + 1] - top), axis=1, keepdims=True)
        total = jnp.where(act_ref[k] > 0, total + seen, total)
    row_lse = top + jnp.log(total)
    row_ref[...] = row_lse
    pack_ref[...] = jnp.zeros_like(pack_ref)
    for k in range(levels + 1):
        tile = tile_ref[k]
        high = jnp.max(tile, axis=0, keepdims=True)
        col = high + jnp.log(jnp.sum(jnp.exp(tile - high), axis=0, keepdims=True))
        if k == 0:
            pack_ref[levels : levels + 1, :] = col
        else:
            pack_ref[k - 1 : k, :] = jnp.where(act_ref[k - 1] > 0, col, ABSENT)
    pack_ref[levels + 1 : levels + 2, :] = as_row(row_lse, rows)
    columns = lax.broadcasted_iota(jnp.int32, (rows, rows), 1)
    picked = jnp.where(pos_ref[...] == columns, tile_ref[0], 0.0)
    picked = jnp.sum(jnp.sum(picked, axis=1, keepdims=True), axis=0, keepdims=True)
    pack_ref[levels + 2 : levels + 3, :] = jnp.broadcast_to(picked, (1, rows))


def grads_kernel(
    levels, act_ref, tile_ref, row_ref, pos_ref, *refs
):
    group = 1 << levels
    packs = refs[:group]
    grad_ref, back_ref, col_ref, far_ref, loss_ref = refs[group:]
    rows = tile_ref.shape[1]

    def columns_of(member):
        terms = [packs[member][levels : levels + 1, :]]
        for k in range(levels):
            terms.append(packs[member ^ 1 << k][k : k + 1, :])
        top = functools.reduce(jnp.maximum, terms)
        return top + jnp.log(sum(jnp.exp(term - top) for term in terms))

    col_lses = [columns_of(member) for member in range(group)]
    loss = jnp.zeros((1, 1), jnp.float32)
    for member in range(group):
        line = col_lses[member] + packs[member][levels + 1 : levels + 2, :]
        loss += jnp.sum(line, axis=1, keepdims=True)
        loss -= 2.0 * packs[member][levels + 2 : levels + 3, 0:1]
    loss_ref[...] = jnp.broadcast_to(loss, loss_ref.shape)

    far_ref[...] = jnp.zeros_like(far_ref)
    col_ref[...] = jnp.zeros_like(col_ref)
    for k in range(levels):
        far = packs[1 << k][levels + 1 : levels + 2, :]
        far = jnp.where(act_ref[k] > 0, far, -ABSENT)
        far_ref[:, k : k + 1] = as_column(far, rows)
        col_ref[k : k + 1, :] = jnp.where(act_ref[k] > 0, col_lses[0], -ABSENT)
    row_lse = row_ref[...]
    own = tile_ref[0]
    columns = lax.broadcasted_iota(jnp.int32, (rows, rows), 1)
    onehot = jnp.where(pos_ref[...] == columns, 2.0, 0.0)
    grad = jnp.exp(own - row_lse) + jnp.exp(own - col_lses[0]) - onehot
    grad_ref[0] = grad.astype(jnp.bfloat16)
    back_ref[...] = grad.T.astype(jnp.bfloat16)
    for k in range(levels):
        tile = tile_ref[k + 1]
        grad = jnp.exp(tile - row_lse) + jnp.exp(tile - col_lses[1 << k])
        grad_ref[k + 1] = jnp.where(act_ref[k] > 0, grad, 0.0).astype(jnp.bfloat16)


def dot(left, right):
    return jnp.dot(left, right, preferred_element_type=jnp.float32)


STEP = 512


def column_blocks(width):
    return [slice(first, first + STEP) for first in range(0, width, STEP)]


def copied_out(buffer_ref, out_ref, sems, j, cols):
    return pltpu.make_async_copy(buffer_ref.at[j], out_ref.at[:, cols], sems.at[j])


def copy_scratch(rows, width):
    steps = width // STEP
    return [pltpu.VMEM((steps, rows, STEP), jnp.float32), pltpu.SemaphoreType.DMA((steps,))]


def query_kernel(count, grad_ref, *refs):
    out_ref, token_ref, buffer_ref, sems = refs[count:]
    token_ref[...] = jnp.zeros_like(token_ref)
    blocks = column_blocks(out_ref.shape[1])
    for j, cols in enumerate(blocks):
        total = dot(grad_ref[0], refs[0][:, cols])
        for k in range(1, count):
            total += dot(grad_ref[k], refs[k][:, cols])
        buffer_ref[j] = total
        copied_out(buffer_ref, out_ref, sems, j, cols).start()
    for j, cols in enumerate(blocks):
        copied_out(buffer_ref, out_ref, sems, j, cols).wait()


def query_product(grads, blocks):
    count, rows, width = len(blocks), *blocks[0].shape
    return call(
        functools.partial(query_kernel, count),
        (f32(rows, width), f32(8, 128)),
        [grads, *blocks],
        out_specs=(
            pl.BlockSpec(memory_space=pl.ANY),
            pl.BlockSpec(memory_space=pltpu.VMEM),
        ),
        scratch_shapes=copy_scratch(rows, width),
    )


def passage_kernel(pieces, last, col_ref, far_ref, *refs):
    count = len(pieces)
    if last:
        stacks, refs = refs[:2], refs[2:]
        parts = [stack.at[n] for n in range(count) for stack in stacks]
    else:
        parts, refs = refs[: 2 * count], refs[2 * count :]
    heads = 1 if last else 2
    head, blocks = refs[:heads], refs[heads : heads + count]
    out_ref, *scratch = refs[heads + count :]
    grads = scratch[:count]
    for n, (k, start) in enumerate(pieces):
        rows = blocks[n].shape[0]
        tile = (parts[2 * n][...] + parts[2 * n + 1][...]) * (1.0 / math.sqrt(D))
        far = far_ref[start : start + rows, k : k + 1]
        grad = jnp.exp(tile - far) + jnp.exp(tile - col_ref[k : k + 1, :])
        grads[n][...] = grad.T.astype(jnp.bfloat16)

    columns = column_blocks(out_ref.shape[1])
    for j, cols in enumerate(columns):
        if last:
            total = head[0][:, cols]
        else:
            total = dot(head[0][...], head[1][:, cols])
        for grad_ref, block in zip(grads, blocks):
            total += dot(grad_ref[...], block[:, cols])
        if last:
            buffer_ref, sems = scratch[count:]
            buffer_ref[j] = total
            copied_out(buffer_ref, out_ref, sems, j, cols).start()
        else:
            out_ref[:, cols] = total
    if last:
        for j, cols in enumerate(columns):
            copied_out(buffer_ref, out_ref, sems, j, cols).wait()


def passage_product(col, far, head, parts, pieces, blocks, last):
    rows, width = far.shape[0], blocks[0].shape[1]
    scratch = [pltpu.VMEM((rows, block.shape[0]), jnp.bfloat16) for block in blocks]
    if last:
        scratch += copy_scratch(rows, width)
    return call(
        functools.partial(passage_kernel, pieces, last),
        f32(rows, width),
        [col, far, *parts, *head, *blocks],
        out_specs=pl.BlockSpec(memory_space=pl.ANY if last else pltpu.VMEM),
        scratch_shapes=scratch,
    )


def local(queries, passages, positive, pair_on):
    rows, _ = queries.shape
    levels = pair_on.shape[1]
    me = lax.axis_index("dp")
    shards = lax.axis_size("dp")
    low = shards.bit_length() - 1 - levels
    masks = [1 << low + k for k in range(levels)]
    active = pair_on[me]
    place = positive.reshape(rows, 1)

    first = 13 * rows // 24
    upper = list(reversed(range(1, levels)))
    far_p = [None] * levels
    for k in reversed(range(levels)):
        far_p[k] = exchanged(passages, "dp", masks[k])
    part = 5 * rows // 6
    far_upper = exchanged(queries[:part], "dp", masks[0])
    far_q = joined(far_upper, exchanged(queries[part:], "dp", masks[0]))
    head = held_until(rows_after(queries, 0, first, []), [far_upper])
    heads = [exchanged(head, "dp", masks[k]) for k in upper]

    early = partial_tiles(queries, [passages, far_p[0]])
    early_other = exchanged(early, "sub", 1)
    late = [
        partial_tiles(queries, [block], [early_other])
        for block in [far_p[k] for k in upper]
    ]
    late_parts = []
    for part in late:
        late_parts += [part, exchanged(part, "sub", 1)]
    (near,) = partial_rows(passages, [far_q])
    near = [near, exchanged(near, "sub", 1)]
    tiles, row_lse, pack = call(
        functools.partial(stats_kernel, levels, [0, 1] + [k + 1 for k in upper], 1),
        (f32(levels + 1, rows, rows), f32(rows, 1), f32(8, rows)),
        [
            active,
            early, early_other,
            *late_parts,
            place,
            near[1],
        ],
        scalars=1,
        unread=1,
    )

    group = 1 << levels
    packs = [None] * group
    packs[0] = pack
    for member in range(3, group, 2):
        offset = sum(masks[k] for k in range(levels) if member >> k & 1)
        packs[member] = exchanged(pack, "dp", offset)
    come = [packs[member | (member > 1)] for member in range(0, group, 2)]
    tails = [
        exchanged(rows_after(queries, first, rows - first, [pack, piece]), "dp", masks[k])
        for k, piece in zip(upper, heads)
    ]
    bundle = call(
        functools.partial(stack_kernel, len(come)),
        f32(len(come), *pack.shape),
        come,
    )
    swapped = exchanged(bundle, "dp", masks[0])
    for n in range(group // 2):
        packs[2 * n if n else 1] = swapped[n]

    grads, back, col_lse, far_lse, total = call(
        functools.partial(grads_kernel, levels),
        (
            bf16(levels + 1, rows, rows),
            bf16(rows, rows),
            f32(8, rows),
            f32(rows, 8),
            f32(8, 128),
        ),
        [active, tiles, row_lse, place, *packs],
        scalars=1,
        flops=4715000000,
    )
    total = total[0, :1]
    for bit in range(low):
        total = total + exchanged(total, "dp", 1 << bit)
    loss = total / (2.0 * rows * shards)

    query_grad, token = query_product(grads, [passages, *far_p])

    parts = near
    for part in partial_rows(passages, heads, [bundle]):
        parts += [part, exchanged(part, "sub", 1)]
    passage_grad = passage_product(
        col_lse,
        far_lse,
        [back, queries],
        parts,
        [(0, 0)] + [(k, 0) for k in upper],
        [far_q, *heads],
        last=False,
    )
    end = partial_stack(passages, tails, [token, passage_grad, loss])
    passage_grad = passage_product(
        col_lse,
        far_lse,
        [passage_grad],
        [end, exchanged(end, "sub", 1)],
        [(k, first) for k in upper],
        tails,
        last=True,
    )
    return (loss, query_grad, passage_grad)


def solution(mesh):
    placed = (P("dp", "sub"), P("dp", "sub"), P("dp", None), P())
    return jax.shard_map(
        local,
        mesh=mesh,
        in_specs=placed,
        out_specs=(P(), P("dp", "sub"), P("dp", "sub")),
        check_vma=False,
    )
```

```python
import functools
import math

import jax
import jax.numpy as jnp
from jax import lax
from jax.experimental import pallas as pl
from jax.experimental.pallas import tpu as pltpu
from jax.sharding import PartitionSpec as P

D = 4096
ABSENT = -1e30


def exchanged(block, axis, offset):
    count = lax.axis_size(axis)
    return lax.ppermute(block, axis, [(i, i ^ offset) for i in range(count)])


def call(kernel, out_shape, operands, **kwargs):
    scalars, unread = kwargs.pop("scalars", 0), kwargs.pop("unread", 0)
    flops = kwargs.pop("flops", 0)
    kwargs["in_specs"] = (
        [pl.BlockSpec(memory_space=pltpu.SMEM)] * scalars
        + [pl.BlockSpec(memory_space=pltpu.VMEM)] * (len(operands) - scalars - unread)
        + [pl.BlockSpec(memory_space=pl.ANY)] * unread
    )
    if "out_specs" not in kwargs:
        kwargs["out_specs"] = jax.tree.map(
            lambda _: pl.BlockSpec(memory_space=pltpu.VMEM), out_shape
        )
    return pl.pallas_call(
        kernel,
        out_shape=out_shape,
        compiler_params=pltpu.CompilerParams(vmem_limit_bytes=12 * 1024 * 1024),
        cost_estimate=pl.CostEstimate(flops=flops, bytes_accessed=0, transcendentals=0),
        **kwargs,
    )(*operands)


def f32(*shape):
    return jax.ShapeDtypeStruct(shape, jnp.float32)


def bf16(*shape):
    return jax.ShapeDtypeStruct(shape, jnp.bfloat16)


def rows_kernel(count, right_ref, *refs):
    for ref, out_ref in zip(refs[:count], refs[-count:]):
        out_ref[...] = lax.dot_general(
            ref[...],
            right_ref[...],
            (((1,), (1,)), ((), ())),
            preferred_element_type=jnp.float32,
        )


def partial_rows(right, blocks, after=()):
    return call(
        functools.partial(rows_kernel, len(blocks)),
        [f32(block.shape[0], right.shape[0]) for block in blocks],
        [right, *blocks, *after],
        unread=len(after),
    )


def stacked_rows_kernel(count, right_ref, *refs):
    for n in range(count):
        refs[-1][n] = lax.dot_general(
            refs[n][...],
            right_ref[...],
            (((1,), (1,)), ((), ())),
            preferred_element_type=jnp.float32,
        )


def partial_stack(right, blocks, after):
    return call(
        functools.partial(stacked_rows_kernel, len(blocks)),
        f32(len(blocks), blocks[0].shape[0], right.shape[0]),
        [right, *blocks, *after],
        unread=len(after),
    )


def tiles_kernel(count, left_ref, *refs):
    out_ref = refs[-1]
    for k, ref in enumerate(refs[:count]):
        out_ref[k] = lax.dot_general(
            left_ref[...],
            ref[...],
            (((1,), (1,)), ((), ())),
            preferred_element_type=jnp.float32,
        )


def partial_tiles(left, blocks, after=()):
    rows, count = left.shape[0], len(blocks)
    return call(
        functools.partial(tiles_kernel, count),
        f32(count, rows, rows),
        [left, *blocks, *after],
        unread=len(after),
    )


def copy_kernel(first, array_ref, *refs):
    refs[-1][...] = array_ref[first : first + refs[-1].shape[0], :]


def rows_after(array, first, count, earlier):
    return call(
        functools.partial(copy_kernel, first),
        jax.ShapeDtypeStruct((count, array.shape[1]), array.dtype),
        [array, *earlier],
        unread=len(earlier),
    )


def pass_kernel(*refs):
    pass


def held_until(array, earlier):
    count = 1 + len(earlier)
    return pl.pallas_call(
        pass_kernel,
        out_shape=jax.ShapeDtypeStruct(array.shape, array.dtype),
        in_specs=[pl.BlockSpec(memory_space=pl.ANY)] * count,
        out_specs=pl.BlockSpec(memory_space=pl.ANY),
        input_output_aliases={0: 0},
        compiler_params=pltpu.CompilerParams(vmem_limit_bytes=1024 * 1024),
        cost_estimate=pl.CostEstimate(flops=0, bytes_accessed=0, transcendentals=0),
    )(array, *earlier)


def join_kernel(upper_ref, lower_ref, out_ref):
    out_ref[: upper_ref.shape[0], :] = upper_ref[...]
    out_ref[upper_ref.shape[0] :, :] = lower_ref[...]


def joined(upper, lower):
    shape = (upper.shape[0] + lower.shape[0], upper.shape[1])
    return call(join_kernel, jax.ShapeDtypeStruct(shape, upper.dtype), [upper, lower])


def stack_kernel(count, *refs):
    for k in range(count):
        refs[-1][k] = refs[k][...]


def as_row(column, rows):
    i = lax.broadcasted_iota(jnp.int32, (rows, rows), 0)
    j = lax.broadcasted_iota(jnp.int32, (rows, rows), 1)
    return jnp.sum(jnp.where(i == j, column, 0.0), axis=0, keepdims=True)


def as_column(row, rows):
    i = lax.broadcasted_iota(jnp.int32, (rows, rows), 0)
    j = lax.broadcasted_iota(jnp.int32, (rows, rows), 1)
    return jnp.sum(jnp.where(i == j, row, 0.0), axis=1, keepdims=True)


def stats_kernel(levels, slots, unread, act_ref, *refs):
    *refs, tile_ref, row_ref, pack_ref = refs
    *part_refs, pos_ref = refs[: len(refs) - unread]
    rows = tile_ref.shape[1]
    scale = 1.0 / math.sqrt(D)
    slots = iter(slots)
    for mine_ref, other_ref in zip(part_refs[0::2], part_refs[1::2]):
        for k in range(mine_ref.shape[0]):
            tile_ref[next(slots)] = (mine_ref[k] + other_ref[k]) * scale
    top = jnp.max(tile_ref[0], axis=1, keepdims=True)
    for k in range(levels):
        seen = jnp.max(tile_ref[k + 1], axis=1, keepdims=True)
        top = jnp.where(act_ref[k] > 0, jnp.maximum(top, seen), top)
    total = jnp.sum(jnp.exp(tile_ref[0] - top), axis=1, keepdims=True)
    for k in range(levels):
        seen = jnp.sum(jnp.exp(tile_ref[k + 1] - top), axis=1, keepdims=True)
        total = jnp.where(act_ref[k] > 0, total + seen, total)
    row_lse = top + jnp.log(total)
    row_ref[...] = row_lse
    pack_ref[...] = jnp.zeros_like(pack_ref)
    for k in range(levels + 1):
        tile = tile_ref[k]
        high = jnp.max(tile, axis=0, keepdims=True)
        col = high + jnp.log(jnp.sum(jnp.exp(tile - high), axis=0, keepdims=True))
        if k == 0:
            pack_ref[levels : levels + 1, :] = col
        else:
            pack_ref[k - 1 : k, :] = jnp.where(act_ref[k - 1] > 0, col, ABSENT)
    pack_ref[levels + 1 : levels + 2, :] = as_row(row_lse, rows)
    columns = lax.broadcasted_iota(jnp.int32, (rows, rows), 1)
    picked = jnp.where(pos_ref[...] == columns, tile_ref[0], 0.0)
    picked = jnp.sum(jnp.sum(picked, axis=1, keepdims=True), axis=0, keepdims=True)
    pack_ref[levels + 2 : levels + 3, :] = jnp.broadcast_to(picked, (1, rows))


def grads_kernel(
    levels, act_ref, tile_ref, row_ref, pos_ref, *refs
):
    group = 1 << levels
    packs = refs[:group]
    grad_ref, back_ref, col_ref, far_ref, loss_ref = refs[group:]
    rows = tile_ref.shape[1]

    def columns_of(member):
        terms = [packs[member][levels : levels + 1, :]]
        for k in range(levels):
            terms.append(packs[member ^ 1 << k][k : k + 1, :])
        top = functools.reduce(jnp.maximum, terms)
        return top + jnp.log(sum(jnp.exp(term - top) for term in terms))

    col_lses = [columns_of(member) for member in range(group)]
    loss = jnp.zeros((1, 1), jnp.float32)
    for member in range(group):
        line = col_lses[member] + packs[member][levels + 1 : levels + 2, :]
        loss += jnp.sum(line, axis=1, keepdims=True)
        loss -= 2.0 * packs[member][levels + 2 : levels + 3, 0:1]
    loss_ref[...] = jnp.broadcast_to(loss, loss_ref.shape)

    far_ref[...] = jnp.zeros_like(far_ref)
    col_ref[...] = jnp.zeros_like(col_ref)
    for k in range(levels):
        far = packs[1 << k][levels + 1 : levels + 2, :]
        far = jnp.where(act_ref[k] > 0, far, -ABSENT)
        far_ref[:, k : k + 1] = as_column(far, rows)
        col_ref[k : k + 1, :] = jnp.where(act_ref[k] > 0, col_lses[0], -ABSENT)
    row_lse = row_ref[...]
    own = tile_ref[0]
    columns = lax.broadcasted_iota(jnp.int32, (rows, rows), 1)
    onehot = jnp.where(pos_ref[...] == columns, 2.0, 0.0)
    grad = jnp.exp(own - row_lse) + jnp.exp(own - col_lses[0]) - onehot
    grad_ref[0] = grad.astype(jnp.bfloat16)
    back_ref[...] = grad.T.astype(jnp.bfloat16)
    for k in range(levels):
        tile = tile_ref[k + 1]
        grad = jnp.exp(tile - row_lse) + jnp.exp(tile - col_lses[1 << k])
        grad_ref[k + 1] = jnp.where(act_ref[k] > 0, grad, 0.0).astype(jnp.bfloat16)


def dot(left, right):
    return jnp.dot(left, right, preferred_element_type=jnp.float32)


STEP = 512


def column_blocks(width):
    return [slice(first, first + STEP) for first in range(0, width, STEP)]


def copied_out(buffer_ref, out_ref, sems, j, cols):
    return pltpu.make_async_copy(buffer_ref.at[j], out_ref.at[:, cols], sems.at[j])


def copy_scratch(rows, width):
    steps = width // STEP
    return [pltpu.VMEM((steps, rows, STEP), jnp.float32), pltpu.SemaphoreType.DMA((steps,))]


def query_kernel(count, grad_ref, *refs):
    out_ref, token_ref, buffer_ref, sems = refs[count:]
    token_ref[...] = jnp.zeros_like(token_ref)
    blocks = column_blocks(out_ref.shape[1])
    for j, cols in enumerate(blocks):
        total = dot(grad_ref[0], refs[0][:, cols])
        for k in range(1, count):
            total += dot(grad_ref[k], refs[k][:, cols])
        buffer_ref[j] = total
        copied_out(buffer_ref, out_ref, sems, j, cols).start()
    for j, cols in enumerate(blocks):
        copied_out(buffer_ref, out_ref, sems, j, cols).wait()


def query_product(grads, blocks):
    count, rows, width = len(blocks), *blocks[0].shape
    return call(
        functools.partial(query_kernel, count),
        (f32(rows, width), f32(8, 128)),
        [grads, *blocks],
        out_specs=(
            pl.BlockSpec(memory_space=pl.ANY),
            pl.BlockSpec(memory_space=pltpu.VMEM),
        ),
        scratch_shapes=copy_scratch(rows, width),
    )


def passage_kernel(pieces, last, col_ref, far_ref, *refs):
    count = len(pieces)
    if last:
        stacks, refs = refs[:2], refs[2:]
        parts = [stack.at[n] for n in range(count) for stack in stacks]
    else:
        parts, refs = refs[: 2 * count], refs[2 * count :]
    heads = 1 if last else 2
    head, blocks = refs[:heads], refs[heads : heads + count]
    out_ref, *scratch = refs[heads + count :]
    grads = scratch[:count]
    for n, (k, start) in enumerate(pieces):
        rows = blocks[n].shape[0]
        tile = (parts[2 * n][...] + parts[2 * n + 1][...]) * (1.0 / math.sqrt(D))
        far = far_ref[start : start + rows, k : k + 1]
        grad = jnp.exp(tile - far) + jnp.exp(tile - col_ref[k : k + 1, :])
        grads[n][...] = grad.T.astype(jnp.bfloat16)

    columns = column_blocks(out_ref.shape[1])
    for j, cols in enumerate(columns):
        if last:
            total = head[0][:, cols]
        else:
            total = dot(head[0][...], head[1][:, cols])
        for grad_ref, block in zip(grads, blocks):
            total += dot(grad_ref[...], block[:, cols])
        if last:
            buffer_ref, sems = scratch[count:]
            buffer_ref[j] = total
            copied_out(buffer_ref, out_ref, sems, j, cols).start()
        else:
            out_ref[:, cols] = total
    if last:
        for j, cols in enumerate(columns):
            copied_out(buffer_ref, out_ref, sems, j, cols).wait()


def passage_product(col, far, head, parts, pieces, blocks, last):
    rows, width = far.shape[0], blocks[0].shape[1]
    scratch = [pltpu.VMEM((rows, block.shape[0]), jnp.bfloat16) for block in blocks]
    if last:
        scratch += copy_scratch(rows, width)
    return call(
        functools.partial(passage_kernel, pieces, last),
        f32(rows, width),
        [col, far, *parts, *head, *blocks],
        out_specs=pl.BlockSpec(memory_space=pl.ANY if last else pltpu.VMEM),
        scratch_shapes=scratch,
    )


def local(queries, passages, positive, pair_on):
    rows, _ = queries.shape
    levels = pair_on.shape[1]
    me = lax.axis_index("dp")
    shards = lax.axis_size("dp")
    low = shards.bit_length() - 1 - levels
    masks = [1 << low + k for k in range(levels)]
    active = pair_on[me]
    place = positive.reshape(rows, 1)

    first = 13 * rows // 24
    upper = list(reversed(range(1, levels)))
    far_p = [None] * levels
    for k in reversed(range(levels)):
        far_p[k] = exchanged(passages, "dp", masks[k])
    part = 5 * rows // 6
    far_upper = exchanged(queries[:part], "dp", masks[0])
    far_q = joined(far_upper, exchanged(queries[part:], "dp", masks[0]))
    head = held_until(rows_after(queries, 0, first, []), [far_upper])
    heads = [exchanged(head, "dp", masks[k]) for k in upper]

    early = partial_tiles(queries, [passages, far_p[0]])
    early_other = exchanged(early, "sub", 1)
    late = [
        partial_tiles(queries, [block], [early_other])
        for block in [far_p[k] for k in upper]
    ]
    late_parts = []
    for part in late:
        late_parts += [part, exchanged(part, "sub", 1)]
    (near,) = partial_rows(passages, [far_q])
    near = [near, exchanged(near, "sub", 1)]
    tiles, row_lse, pack = call(
        functools.partial(stats_kernel, levels, [0, 1] + [k + 1 for k in upper], 1),
        (f32(levels + 1, rows, rows), f32(rows, 1), f32(8, rows)),
        [
            active,
            early, early_other,
            *late_parts,
            place,
            near[1],
        ],
        scalars=1,
        unread=1,
    )

    group = 1 << levels
    packs = [None] * group
    packs[0] = pack
    for member in range(3, group, 2):
        offset = sum(masks[k] for k in range(levels) if member >> k & 1)
        packs[member] = exchanged(pack, "dp", offset)
    come = [packs[member | (member > 1)] for member in range(0, group, 2)]
    tails = [
        exchanged(rows_after(queries, first, rows - first, [pack, piece]), "dp", masks[k])
        for k, piece in zip(upper, heads)
    ]
    bundle = call(
        functools.partial(stack_kernel, len(come)),
        f32(len(come), *pack.shape),
        come,
    )
    swapped = exchanged(bundle, "dp", masks[0])
    for n in range(group // 2):
        packs[2 * n if n else 1] = swapped[n]

    grads, back, col_lse, far_lse, total = call(
        functools.partial(grads_kernel, levels),
        (
            bf16(levels + 1, rows, rows),
            bf16(rows, rows),
            f32(8, rows),
            f32(rows, 8),
            f32(8, 128),
        ),
        [active, tiles, row_lse, place, *packs],
        scalars=1,
        flops=4715000000,
    )
    total = total[0, :1]
    for bit in range(low):
        total = total + exchanged(total, "dp", 1 << bit)
    loss = total / (2.0 * rows * shards)

    query_grad, token = query_product(grads, [passages, *far_p])

    parts = near
    for part in partial_rows(passages, heads, [bundle]):
        parts += [part, exchanged(part, "sub", 1)]
    passage_grad = passage_product(
        col_lse,
        far_lse,
        [back, queries],
        parts,
        [(0, 0)] + [(k, 0) for k in upper],
        [far_q, *heads],
        last=False,
    )
    end = partial_stack(passages, tails, [token, passage_grad, loss])
    passage_grad = passage_product(
        col_lse,
        far_lse,
        [passage_grad],
        [end, exchanged(end, "sub", 1)],
        [(k, first) for k in upper],
        tails,
        last=True,
    )
    return (loss, query_grad, passage_grad)


def solution(mesh):
    placed = (P("dp", "sub"), P("dp", "sub"), P("dp", None), P())
    return jax.shard_map(
        local,
        mesh=mesh,
        in_specs=placed,
        out_specs=(P(), P("dp", "sub"), P("dp", "sub")),
        check_vma=False,
    )
```

```python
import functools
import math

import jax
import jax.numpy as jnp
from jax import lax
from jax.experimental import pallas as pl
from jax.experimental.pallas import tpu as pltpu
from jax.sharding import PartitionSpec as P

D = 4096
ABSENT = -1e30


def exchanged(block, axis, offset):
    count = lax.axis_size(axis)
    return lax.ppermute(block, axis, [(i, i ^ offset) for i in range(count)])


def call(kernel, out_shape, operands, **kwargs):
    scalars, unread = kwargs.pop("scalars", 0), kwargs.pop("unread", 0)
    flops = kwargs.pop("flops", 0)
    kwargs["in_specs"] = (
        [pl.BlockSpec(memory_space=pltpu.SMEM)] * scalars
        + [pl.BlockSpec(memory_space=pltpu.VMEM)] * (len(operands) - scalars - unread)
        + [pl.BlockSpec(memory_space=pl.ANY)] * unread
    )
    if "out_specs" not in kwargs:
        kwargs["out_specs"] = jax.tree.map(
            lambda _: pl.BlockSpec(memory_space=pltpu.VMEM), out_shape
        )
    return pl.pallas_call(
        kernel,
        out_shape=out_shape,
        compiler_params=pltpu.CompilerParams(vmem_limit_bytes=12 * 1024 * 1024),
        cost_estimate=pl.CostEstimate(flops=flops, bytes_accessed=0, transcendentals=0),
        **kwargs,
    )(*operands)


def f32(*shape):
    return jax.ShapeDtypeStruct(shape, jnp.float32)


def bf16(*shape):
    return jax.ShapeDtypeStruct(shape, jnp.bfloat16)


def rows_kernel(count, right_ref, *refs):
    for ref, out_ref in zip(refs[:count], refs[-count:]):
        out_ref[...] = lax.dot_general(
            ref[...],
            right_ref[...],
            (((1,), (1,)), ((), ())),
            preferred_element_type=jnp.float32,
        )


def partial_rows(right, blocks, after=()):
    return call(
        functools.partial(rows_kernel, len(blocks)),
        [f32(block.shape[0], right.shape[0]) for block in blocks],
        [right, *blocks, *after],
        unread=len(after),
    )


def tiles_kernel(count, left_ref, *refs):
    out_ref = refs[-1]
    for k, ref in enumerate(refs[:count]):
        out_ref[k] = lax.dot_general(
            left_ref[...],
            ref[...],
            (((1,), (1,)), ((), ())),
            preferred_element_type=jnp.float32,
        )


def partial_tiles(left, blocks, after=()):
    rows, count = left.shape[0], len(blocks)
    return call(
        functools.partial(tiles_kernel, count),
        f32(count, rows, rows),
        [left, *blocks, *after],
        unread=len(after),
    )


def copy_kernel(first, array_ref, *refs):
    refs[-1][...] = array_ref[first : first + refs[-1].shape[0], :]


def rows_after(array, first, count, earlier):
    return call(
        functools.partial(copy_kernel, first),
        jax.ShapeDtypeStruct((count, array.shape[1]), array.dtype),
        [array, *earlier],
        unread=len(earlier),
    )


def pass_kernel(*refs):
    pass


def held_until(array, earlier):
    count = 1 + len(earlier)
    return pl.pallas_call(
        pass_kernel,
        out_shape=jax.ShapeDtypeStruct(array.shape, array.dtype),
        in_specs=[pl.BlockSpec(memory_space=pl.ANY)] * count,
        out_specs=pl.BlockSpec(memory_space=pl.ANY),
        input_output_aliases={0: 0},
        compiler_params=pltpu.CompilerParams(vmem_limit_bytes=1024 * 1024),
        cost_estimate=pl.CostEstimate(flops=0, bytes_accessed=0, transcendentals=0),
    )(array, *earlier)


def join_kernel(upper_ref, lower_ref, out_ref):
    out_ref[: upper_ref.shape[0], :] = upper_ref[...]
    out_ref[upper_ref.shape[0] :, :] = lower_ref[...]


def joined(upper, lower):
    shape = (upper.shape[0] + lower.shape[0], upper.shape[1])
    return call(join_kernel, jax.ShapeDtypeStruct(shape, upper.dtype), [upper, lower])


def stack_kernel(count, *refs):
    for k in range(count):
        refs[-1][k] = refs[k][...]


def as_row(column, rows):
    i = lax.broadcasted_iota(jnp.int32, (rows, rows), 0)
    j = lax.broadcasted_iota(jnp.int32, (rows, rows), 1)
    return jnp.sum(jnp.where(i == j, column, 0.0), axis=0, keepdims=True)


def as_column(row, rows):
    i = lax.broadcasted_iota(jnp.int32, (rows, rows), 0)
    j = lax.broadcasted_iota(jnp.int32, (rows, rows), 1)
    return jnp.sum(jnp.where(i == j, row, 0.0), axis=1, keepdims=True)


def stats_kernel(levels, slots, unread, act_ref, *refs):
    *refs, tile_ref, row_ref, pack_ref = refs
    *part_refs, pos_ref = refs[: len(refs) - unread]
    rows = tile_ref.shape[1]
    scale = 1.0 / math.sqrt(D)
    slots = iter(slots)
    for mine_ref, other_ref in zip(part_refs[0::2], part_refs[1::2]):
        for k in range(mine_ref.shape[0]):
            tile_ref[next(slots)] = (mine_ref[k] + other_ref[k]) * scale
    top = jnp.max(tile_ref[0], axis=1, keepdims=True)
    for k in range(levels):
        seen = jnp.max(tile_ref[k + 1], axis=1, keepdims=True)
        top = jnp.where(act_ref[k] > 0, jnp.maximum(top, seen), top)
    total = jnp.sum(jnp.exp(tile_ref[0] - top), axis=1, keepdims=True)
    for k in range(levels):
        seen = jnp.sum(jnp.exp(tile_ref[k + 1] - top), axis=1, keepdims=True)
        total = jnp.where(act_ref[k] > 0, total + seen, total)
    row_lse = top + jnp.log(total)
    row_ref[...] = row_lse
    pack_ref[...] = jnp.zeros_like(pack_ref)
    for k in range(levels + 1):
        tile = tile_ref[k]
        high = jnp.max(tile, axis=0, keepdims=True)
        col = high + jnp.log(jnp.sum(jnp.exp(tile - high), axis=0, keepdims=True))
        if k == 0:
            pack_ref[levels : levels + 1, :] = col
        else:
            pack_ref[k - 1 : k, :] = jnp.where(act_ref[k - 1] > 0, col, ABSENT)
    pack_ref[levels + 1 : levels + 2, :] = as_row(row_lse, rows)
    columns = lax.broadcasted_iota(jnp.int32, (rows, rows), 1)
    picked = jnp.where(pos_ref[...] == columns, tile_ref[0], 0.0)
    picked = jnp.sum(jnp.sum(picked, axis=1, keepdims=True), axis=0, keepdims=True)
    pack_ref[levels + 2 : levels + 3, :] = jnp.broadcast_to(picked, (1, rows))


def grads_kernel(
    levels, act_ref, tile_ref, row_ref, pos_ref, *refs
):
    group = 1 << levels
    packs = refs[:group]
    grad_ref, back_ref, col_ref, far_ref, loss_ref = refs[group:]
    rows = tile_ref.shape[1]

    def columns_of(member):
        terms = [packs[member][levels : levels + 1, :]]
        for k in range(levels):
            terms.append(packs[member ^ 1 << k][k : k + 1, :])
        top = functools.reduce(jnp.maximum, terms)
        return top + jnp.log(sum(jnp.exp(term - top) for term in terms))

    col_lses = [columns_of(member) for member in range(group)]
    loss = jnp.zeros((1, 1), jnp.float32)
    for member in range(group):
        line = col_lses[member] + packs[member][levels + 1 : levels + 2, :]
        loss += jnp.sum(line, axis=1, keepdims=True)
        loss -= 2.0 * packs[member][levels + 2 : levels + 3, 0:1]
    loss_ref[...] = jnp.broadcast_to(loss, loss_ref.shape)

    far_ref[...] = jnp.zeros_like(far_ref)
    col_ref[...] = jnp.zeros_like(col_ref)
    for k in range(levels):
        far = packs[1 << k][levels + 1 : levels + 2, :]
        far = jnp.where(act_ref[k] > 0, far, -ABSENT)
        far_ref[:, k : k + 1] = as_column(far, rows)
        col_ref[k : k + 1, :] = jnp.where(act_ref[k] > 0, col_lses[0], -ABSENT)
    row_lse = row_ref[...]
    own = tile_ref[0]
    columns = lax.broadcasted_iota(jnp.int32, (rows, rows), 1)
    onehot = jnp.where(pos_ref[...] == columns, 2.0, 0.0)
    grad = jnp.exp(own - row_lse) + jnp.exp(own - col_lses[0]) - onehot
    grad_ref[0] = grad.astype(jnp.bfloat16)
    back_ref[...] = grad.T.astype(jnp.bfloat16)
    for k in range(levels):
        tile = tile_ref[k + 1]
        grad = jnp.exp(tile - row_lse) + jnp.exp(tile - col_lses[1 << k])
        grad_ref[k + 1] = jnp.where(act_ref[k] > 0, grad, 0.0).astype(jnp.bfloat16)


def dot(left, right):
    return jnp.dot(left, right, preferred_element_type=jnp.float32)


STEP = 512


def column_blocks(width):
    return [slice(first, first + STEP) for first in range(0, width, STEP)]


def copied_out(buffer_ref, out_ref, sems, j, cols):
    return pltpu.make_async_copy(buffer_ref.at[j], out_ref.at[:, cols], sems.at[j])


def copy_scratch(rows, width):
    steps = width // STEP
    return [pltpu.VMEM((steps, rows, STEP), jnp.float32), pltpu.SemaphoreType.DMA((steps,))]


def query_kernel(count, grad_ref, *refs):
    out_ref, token_ref, buffer_ref, sems = refs[count:]
    token_ref[...] = jnp.zeros_like(token_ref)
    blocks = column_blocks(out_ref.shape[1])
    for j, cols in enumerate(blocks):
        total = dot(grad_ref[0], refs[0][:, cols])
        for k in range(1, count):
            total += dot(grad_ref[k], refs[k][:, cols])
        buffer_ref[j] = total
        copied_out(buffer_ref, out_ref, sems, j, cols).start()
    for j, cols in enumerate(blocks):
        copied_out(buffer_ref, out_ref, sems, j, cols).wait()


def query_product(grads, blocks):
    count, rows, width = len(blocks), *blocks[0].shape
    return call(
        functools.partial(query_kernel, count),
        (f32(rows, width), f32(8, 128)),
        [grads, *blocks],
        out_specs=(
            pl.BlockSpec(memory_space=pl.ANY),
            pl.BlockSpec(memory_space=pltpu.VMEM),
        ),
        scratch_shapes=copy_scratch(rows, width),
    )


def passage_kernel(pieces, last, col_ref, far_ref, *refs):
    count = len(pieces)
    parts, refs = refs[: 2 * count], refs[2 * count :]
    heads = 1 if last else 2
    head, blocks = refs[:heads], refs[heads : heads + count]
    out_ref, *scratch = refs[heads + count :]
    grads = scratch[:count]
    for n, (k, start) in enumerate(pieces):
        rows = blocks[n].shape[0]
        tile = (parts[2 * n][...] + parts[2 * n + 1][...]) * (1.0 / math.sqrt(D))
        far = far_ref[start : start + rows, k : k + 1]
        grad = jnp.exp(tile - far) + jnp.exp(tile - col_ref[k : k + 1, :])
        grads[n][...] = grad.T.astype(jnp.bfloat16)

    columns = column_blocks(out_ref.shape[1])
    for j, cols in enumerate(columns):
        if last:
            total = head[0][:, cols]
        else:
            total = dot(head[0][...], head[1][:, cols])
        for grad_ref, block in zip(grads, blocks):
            total += dot(grad_ref[...], block[:, cols])
        if last:
            buffer_ref, sems = scratch[count:]
            buffer_ref[j] = total
            copied_out(buffer_ref, out_ref, sems, j, cols).start()
        else:
            out_ref[:, cols] = total
    if last:
        for j, cols in enumerate(columns):
            copied_out(buffer_ref, out_ref, sems, j, cols).wait()


def passage_product(col, far, head, parts, pieces, blocks, last):
    rows, width = far.shape[0], blocks[0].shape[1]
    scratch = [pltpu.VMEM((rows, block.shape[0]), jnp.bfloat16) for block in blocks]
    if last:
        scratch += copy_scratch(rows, width)
    return call(
        functools.partial(passage_kernel, pieces, last),
        f32(rows, width),
        [col, far, *parts, *head, *blocks],
        out_specs=pl.BlockSpec(memory_space=pl.ANY if last else pltpu.VMEM),
        scratch_shapes=scratch,
    )


def local(queries, passages, positive, pair_on):
    rows, _ = queries.shape
    levels = pair_on.shape[1]
    me = lax.axis_index("dp")
    shards = lax.axis_size("dp")
    low = shards.bit_length() - 1 - levels
    masks = [1 << low + k for k in range(levels)]
    active = pair_on[me]
    place = positive.reshape(rows, 1)

    first = 13 * rows // 24
    upper = list(reversed(range(1, levels)))
    far_p = [None] * levels
    for k in reversed(range(levels)):
        far_p[k] = exchanged(passages, "dp", masks[k])
    part = 3 * rows // 4
    far_upper = exchanged(queries[:part], "dp", masks[0])
    far_q = joined(far_upper, exchanged(queries[part:], "dp", masks[0]))
    firsts = {upper[0]: first, upper[1]: 5 * rows // 8}
    heads = []
    for k in upper:
        head = held_until(rows_after(queries, 0, firsts[k], []), [far_upper])
        heads.append(exchanged(head, "dp", masks[k]))

    early = partial_tiles(queries, [passages, far_p[0]])
    early_other = exchanged(early, "sub", 1)
    late = [
        partial_tiles(queries, [block], [early_other])
        for block in [far_p[k] for k in upper]
    ]
    late_parts = []
    for part in late:
        late_parts += [part, exchanged(part, "sub", 1)]
    (near,) = partial_rows(passages, [far_q])
    near = [near, exchanged(near, "sub", 1)]
    tiles, row_lse, pack = call(
        functools.partial(stats_kernel, levels, [0, 1] + [k + 1 for k in upper], 1),
        (f32(levels + 1, rows, rows), f32(rows, 1), f32(8, rows)),
        [
            active,
            early, early_other,
            *late_parts,
            place,
            near[1],
        ],
        scalars=1,
        unread=1,
    )

    group = 1 << levels
    packs = [None] * group
    packs[0] = pack
    for member in range(3, group, 2):
        offset = sum(masks[k] for k in range(levels) if member >> k & 1)
        packs[member] = exchanged(pack, "dp", offset)
    come = [packs[member | (member > 1)] for member in range(0, group, 2)]
    tails = [
        exchanged(
            rows_after(queries, firsts[k], rows - firsts[k], [pack, piece]), "dp", masks[k]
        )
        for k, piece in zip(upper, heads)
    ]
    bundle = call(
        functools.partial(stack_kernel, len(come)),
        f32(len(come), *pack.shape),
        come,
    )
    swapped = exchanged(bundle, "dp", masks[0])
    for n in range(group // 2):
        packs[2 * n if n else 1] = swapped[n]

    grads, back, col_lse, far_lse, total = call(
        functools.partial(grads_kernel, levels),
        (
            bf16(levels + 1, rows, rows),
            bf16(rows, rows),
            f32(8, rows),
            f32(rows, 8),
            f32(8, 128),
        ),
        [active, tiles, row_lse, place, *packs],
        scalars=1,
        flops=4692000000,
    )
    total = total[0, :1]
    for bit in range(low):
        total = total + exchanged(total, "dp", 1 << bit)
    loss = total / (2.0 * rows * shards)

    query_grad, token = query_product(grads, [passages, *far_p])

    parts = near
    for part in partial_rows(passages, heads, [bundle]):
        parts += [part, exchanged(part, "sub", 1)]
    passage_grad = passage_product(
        col_lse,
        far_lse,
        [back, queries],
        parts,
        [(0, 0)] + [(k, 0) for k in upper],
        [far_q, *heads],
        last=False,
    )
    ends = []
    for piece in tails[::-1]:
        (part,) = partial_rows(passages, [piece], ends[-2:-1] or [token, passage_grad, loss])
        ends += [part, exchanged(part, "sub", 1)]
    passage_grad = passage_product(
        col_lse,
        far_lse,
        [passage_grad],
        ends,
        [(k, firsts[k]) for k in upper[::-1]],
        tails[::-1],
        last=True,
    )
    return (loss, query_grad, passage_grad)


def solution(mesh):
    placed = (P("dp", "sub"), P("dp", "sub"), P("dp", None), P())
    return jax.shard_map(
        local,
        mesh=mesh,
        in_specs=placed,
        out_specs=(P(), P("dp", "sub"), P("dp", "sub")),
        check_vma=False,
    )
```

```python
import functools
import math

import jax
import jax.numpy as jnp
from jax import lax
from jax.experimental import pallas as pl
from jax.experimental.pallas import tpu as pltpu
from jax.sharding import PartitionSpec as P

D = 4096
ABSENT = -1e30


def exchanged(block, axis, offset):
    count = lax.axis_size(axis)
    return lax.ppermute(block, axis, [(i, i ^ offset) for i in range(count)])


def call(kernel, out_shape, operands, **kwargs):
    scalars, unread = kwargs.pop("scalars", 0), kwargs.pop("unread", 0)
    flops = kwargs.pop("flops", 0)
    kwargs["in_specs"] = (
        [pl.BlockSpec(memory_space=pltpu.SMEM)] * scalars
        + [pl.BlockSpec(memory_space=pltpu.VMEM)] * (len(operands) - scalars - unread)
        + [pl.BlockSpec(memory_space=pl.ANY)] * unread
    )
    if "out_specs" not in kwargs:
        kwargs["out_specs"] = jax.tree.map(
            lambda _: pl.BlockSpec(memory_space=pltpu.VMEM), out_shape
        )
    return pl.pallas_call(
        kernel,
        out_shape=out_shape,
        compiler_params=pltpu.CompilerParams(vmem_limit_bytes=12 * 1024 * 1024),
        cost_estimate=pl.CostEstimate(flops=flops, bytes_accessed=0, transcendentals=0),
        **kwargs,
    )(*operands)


def f32(*shape):
    return jax.ShapeDtypeStruct(shape, jnp.float32)


def bf16(*shape):
    return jax.ShapeDtypeStruct(shape, jnp.bfloat16)


def rows_kernel(count, right_ref, *refs):
    for ref, out_ref in zip(refs[:count], refs[-count:]):
        out_ref[...] = lax.dot_general(
            ref[...],
            right_ref[...],
            (((1,), (1,)), ((), ())),
            preferred_element_type=jnp.float32,
        )


def partial_rows(right, blocks, after=()):
    return call(
        functools.partial(rows_kernel, len(blocks)),
        [f32(block.shape[0], right.shape[0]) for block in blocks],
        [right, *blocks, *after],
        unread=len(after),
    )


def stacked_rows_kernel(count, right_ref, *refs):
    for n in range(count):
        refs[-1][n] = lax.dot_general(
            refs[n][...],
            right_ref[...],
            (((1,), (1,)), ((), ())),
            preferred_element_type=jnp.float32,
        )


def partial_stack(right, blocks, after):
    return call(
        functools.partial(stacked_rows_kernel, len(blocks)),
        f32(len(blocks), blocks[0].shape[0], right.shape[0]),
        [right, *blocks, *after],
        unread=len(after),
    )


def tiles_kernel(count, left_ref, *refs):
    out_ref = refs[-1]
    for k, ref in enumerate(refs[:count]):
        out_ref[k] = lax.dot_general(
            left_ref[...],
            ref[...],
            (((1,), (1,)), ((), ())),
            preferred_element_type=jnp.float32,
        )


def partial_tiles(left, blocks, after=()):
    rows, count = left.shape[0], len(blocks)
    return call(
        functools.partial(tiles_kernel, count),
        f32(count, rows, rows),
        [left, *blocks, *after],
        unread=len(after),
    )


def copy_kernel(first, array_ref, *refs):
    refs[-1][...] = array_ref[first : first + refs[-1].shape[0], :]


def rows_after(array, first, count, earlier):
    return call(
        functools.partial(copy_kernel, first),
        jax.ShapeDtypeStruct((count, array.shape[1]), array.dtype),
        [array, *earlier],
        unread=len(earlier),
    )


def pass_kernel(*refs):
    pass


def held_until(array, earlier):
    count = 1 + len(earlier)
    return pl.pallas_call(
        pass_kernel,
        out_shape=jax.ShapeDtypeStruct(array.shape, array.dtype),
        in_specs=[pl.BlockSpec(memory_space=pl.ANY)] * count,
        out_specs=pl.BlockSpec(memory_space=pl.ANY),
        input_output_aliases={0: 0},
        compiler_params=pltpu.CompilerParams(vmem_limit_bytes=1024 * 1024),
        cost_estimate=pl.CostEstimate(flops=0, bytes_accessed=0, transcendentals=0),
    )(array, *earlier)


def join_kernel(upper_ref, lower_ref, out_ref):
    out_ref[: upper_ref.shape[0], :] = upper_ref[...]
    out_ref[upper_ref.shape[0] :, :] = lower_ref[...]


def joined(upper, lower):
    shape = (upper.shape[0] + lower.shape[0], upper.shape[1])
    return call(join_kernel, jax.ShapeDtypeStruct(shape, upper.dtype), [upper, lower])


def stack_kernel(count, *refs):
    for k in range(count):
        refs[-1][k] = refs[k][...]


def as_row(column, rows):
    i = lax.broadcasted_iota(jnp.int32, (rows, rows), 0)
    j = lax.broadcasted_iota(jnp.int32, (rows, rows), 1)
    return jnp.sum(jnp.where(i == j, column, 0.0), axis=0, keepdims=True)


def as_column(row, rows):
    i = lax.broadcasted_iota(jnp.int32, (rows, rows), 0)
    j = lax.broadcasted_iota(jnp.int32, (rows, rows), 1)
    return jnp.sum(jnp.where(i == j, row, 0.0), axis=1, keepdims=True)


def stats_kernel(levels, slots, unread, act_ref, *refs):
    *refs, tile_ref, row_ref, pack_ref = refs
    *part_refs, pos_ref = refs[: len(refs) - unread]
    rows = tile_ref.shape[1]
    scale = 1.0 / math.sqrt(D)
    slots = iter(slots)
    for mine_ref, other_ref in zip(part_refs[0::2], part_refs[1::2]):
        for k in range(mine_ref.shape[0]):
            tile_ref[next(slots)] = (mine_ref[k] + other_ref[k]) * scale
    top = jnp.max(tile_ref[0], axis=1, keepdims=True)
    for k in range(levels):
        seen = jnp.max(tile_ref[k + 1], axis=1, keepdims=True)
        top = jnp.where(act_ref[k] > 0, jnp.maximum(top, seen), top)
    total = jnp.sum(jnp.exp(tile_ref[0] - top), axis=1, keepdims=True)
    for k in range(levels):
        seen = jnp.sum(jnp.exp(tile_ref[k + 1] - top), axis=1, keepdims=True)
        total = jnp.where(act_ref[k] > 0, total + seen, total)
    row_lse = top + jnp.log(total)
    row_ref[...] = row_lse
    pack_ref[...] = jnp.zeros_like(pack_ref)
    for k in range(levels + 1):
        tile = tile_ref[k]
        high = jnp.max(tile, axis=0, keepdims=True)
        col = high + jnp.log(jnp.sum(jnp.exp(tile - high), axis=0, keepdims=True))
        if k == 0:
            pack_ref[levels : levels + 1, :] = col
        else:
            pack_ref[k - 1 : k, :] = jnp.where(act_ref[k - 1] > 0, col, ABSENT)
    pack_ref[levels + 1 : levels + 2, :] = as_row(row_lse, rows)
    columns = lax.broadcasted_iota(jnp.int32, (rows, rows), 1)
    picked = jnp.where(pos_ref[...] == columns, tile_ref[0], 0.0)
    picked = jnp.sum(jnp.sum(picked, axis=1, keepdims=True), axis=0, keepdims=True)
    pack_ref[levels + 2 : levels + 3, :] = jnp.broadcast_to(picked, (1, rows))


def grads_kernel(
    levels, act_ref, tile_ref, row_ref, pos_ref, *refs
):
    group = 1 << levels
    packs = refs[:group]
    grad_ref, back_ref, col_ref, far_ref, loss_ref = refs[group:]
    rows = tile_ref.shape[1]

    def columns_of(member):
        terms = [packs[member][levels : levels + 1, :]]
        for k in range(levels):
            terms.append(packs[member ^ 1 << k][k : k + 1, :])
        top = functools.reduce(jnp.maximum, terms)
        return top + jnp.log(sum(jnp.exp(term - top) for term in terms))

    col_lses = [columns_of(member) for member in range(group)]
    loss = jnp.zeros((1, 1), jnp.float32)
    for member in range(group):
        line = col_lses[member] + packs[member][levels + 1 : levels + 2, :]
        loss += jnp.sum(line, axis=1, keepdims=True)
        loss -= 2.0 * packs[member][levels + 2 : levels + 3, 0:1]
    loss_ref[...] = jnp.broadcast_to(loss, loss_ref.shape)

    far_ref[...] = jnp.zeros_like(far_ref)
    col_ref[...] = jnp.zeros_like(col_ref)
    for k in range(levels):
        far = packs[1 << k][levels + 1 : levels + 2, :]
        far = jnp.where(act_ref[k] > 0, far, -ABSENT)
        far_ref[:, k : k + 1] = as_column(far, rows)
        col_ref[k : k + 1, :] = jnp.where(act_ref[k] > 0, col_lses[0], -ABSENT)
    row_lse = row_ref[...]
    own = tile_ref[0]
    columns = lax.broadcasted_iota(jnp.int32, (rows, rows), 1)
    onehot = jnp.where(pos_ref[...] == columns, 2.0, 0.0)
    grad = jnp.exp(own - row_lse) + jnp.exp(own - col_lses[0]) - onehot
    grad_ref[0] = grad.astype(jnp.bfloat16)
    back_ref[...] = grad.T.astype(jnp.bfloat16)
    for k in range(levels):
        tile = tile_ref[k + 1]
        grad = jnp.exp(tile - row_lse) + jnp.exp(tile - col_lses[1 << k])
        grad_ref[k + 1] = jnp.where(act_ref[k] > 0, grad, 0.0).astype(jnp.bfloat16)


def dot(left, right):
    return jnp.dot(left, right, preferred_element_type=jnp.float32)


STEP = 512


def column_blocks(width):
    return [slice(first, first + STEP) for first in range(0, width, STEP)]


def copied_out(buffer_ref, out_ref, sems, j, cols):
    return pltpu.make_async_copy(buffer_ref.at[j], out_ref.at[:, cols], sems.at[j])


def copy_scratch(rows, width):
    steps = width // STEP
    return [pltpu.VMEM((steps, rows, STEP), jnp.float32), pltpu.SemaphoreType.DMA((steps,))]


def query_kernel(count, grad_ref, *refs):
    out_ref, token_ref, buffer_ref, sems = refs[count:]
    token_ref[...] = jnp.zeros_like(token_ref)
    blocks = column_blocks(out_ref.shape[1])
    for j, cols in enumerate(blocks):
        total = dot(grad_ref[0], refs[0][:, cols])
        for k in range(1, count):
            total += dot(grad_ref[k], refs[k][:, cols])
        buffer_ref[j] = total
        copied_out(buffer_ref, out_ref, sems, j, cols).start()
    for j, cols in enumerate(blocks):
        copied_out(buffer_ref, out_ref, sems, j, cols).wait()


def query_product(grads, blocks):
    count, rows, width = len(blocks), *blocks[0].shape
    return call(
        functools.partial(query_kernel, count),
        (f32(rows, width), f32(8, 128)),
        [grads, *blocks],
        out_specs=(
            pl.BlockSpec(memory_space=pl.ANY),
            pl.BlockSpec(memory_space=pltpu.VMEM),
        ),
        scratch_shapes=copy_scratch(rows, width),
    )


def passage_kernel(pieces, last, col_ref, far_ref, *refs):
    count = len(pieces)
    if last:
        stacks, refs = refs[:2], refs[2:]
        parts = [stack.at[n] for n in range(count) for stack in stacks]
    else:
        parts, refs = refs[: 2 * count], refs[2 * count :]
    heads = 1 if last else 2
    head, blocks = refs[:heads], refs[heads : heads + count]
    out_ref, *scratch = refs[heads + count :]
    grads = scratch[:count]
    for n, (k, start) in enumerate(pieces):
        rows = blocks[n].shape[0]
        tile = (parts[2 * n][...] + parts[2 * n + 1][...]) * (1.0 / math.sqrt(D))
        far = far_ref[start : start + rows, k : k + 1]
        grad = jnp.exp(tile - far) + jnp.exp(tile - col_ref[k : k + 1, :])
        grads[n][...] = grad.T.astype(jnp.bfloat16)

    columns = column_blocks(out_ref.shape[1])
    for j, cols in enumerate(columns):
        if last:
            total = head[0][:, cols]
        else:
            total = dot(head[0][...], head[1][:, cols])
        for grad_ref, block in zip(grads, blocks):
            total += dot(grad_ref[...], block[:, cols])
        if last:
            buffer_ref, sems = scratch[count:]
            buffer_ref[j] = total
            copied_out(buffer_ref, out_ref, sems, j, cols).start()
        else:
            out_ref[:, cols] = total
    if last:
        for j, cols in enumerate(columns):
            copied_out(buffer_ref, out_ref, sems, j, cols).wait()


def passage_product(col, far, head, parts, pieces, blocks, last):
    rows, width = far.shape[0], blocks[0].shape[1]
    scratch = [pltpu.VMEM((rows, block.shape[0]), jnp.bfloat16) for block in blocks]
    if last:
        scratch += copy_scratch(rows, width)
    return call(
        functools.partial(passage_kernel, pieces, last),
        f32(rows, width),
        [col, far, *parts, *head, *blocks],
        out_specs=pl.BlockSpec(memory_space=pl.ANY if last else pltpu.VMEM),
        scratch_shapes=scratch,
    )


def local(queries, passages, positive, pair_on):
    rows, _ = queries.shape
    levels = pair_on.shape[1]
    me = lax.axis_index("dp")
    shards = lax.axis_size("dp")
    low = shards.bit_length() - 1 - levels
    masks = [1 << low + k for k in range(levels)]
    active = pair_on[me]
    place = positive.reshape(rows, 1)

    first = 13 * rows // 24
    upper = list(reversed(range(1, levels)))
    far_p = [None] * levels
    for k in reversed(range(levels)):
        far_p[k] = exchanged(passages, "dp", masks[k])
    part = 2 * rows // 3
    far_upper = exchanged(queries[:part], "dp", masks[0])
    far_q = joined(far_upper, exchanged(queries[part:], "dp", masks[0]))
    head = held_until(rows_after(queries, 0, first, []), [far_upper])
    heads = [exchanged(head, "dp", masks[k]) for k in upper]

    early = partial_tiles(queries, [passages, far_p[0]])
    early_other = exchanged(early, "sub", 1)
    late = [
        partial_tiles(queries, [block], [early_other])
        for block in [far_p[k] for k in upper]
    ]
    late_parts = []
    for part in late:
        late_parts += [part, exchanged(part, "sub", 1)]
    (near,) = partial_rows(passages, [far_q])
    near = [near, exchanged(near, "sub", 1)]
    tiles, row_lse, pack = call(
        functools.partial(stats_kernel, levels, [0, 1] + [k + 1 for k in upper], 1),
        (f32(levels + 1, rows, rows), f32(rows, 1), f32(8, rows)),
        [
            active,
            early, early_other,
            *late_parts,
            place,
            near[1],
        ],
        scalars=1,
        unread=1,
    )

    group = 1 << levels
    packs = [None] * group
    packs[0] = pack
    for member in range(3, group, 2):
        offset = sum(masks[k] for k in range(levels) if member >> k & 1)
        packs[member] = exchanged(pack, "dp", offset)
    come = [packs[member | (member > 1)] for member in range(0, group, 2)]
    tails = [
        exchanged(rows_after(queries, first, rows - first, [pack, piece]), "dp", masks[k])
        for k, piece in zip(upper, heads)
    ]
    bundle = call(
        functools.partial(stack_kernel, len(come)),
        f32(len(come), *pack.shape),
        come,
    )
    swapped = exchanged(bundle, "dp", masks[0])
    for n in range(group // 2):
        packs[2 * n if n else 1] = swapped[n]

    grads, back, col_lse, far_lse, total = call(
        functools.partial(grads_kernel, levels),
        (
            bf16(levels + 1, rows, rows),
            bf16(rows, rows),
            f32(8, rows),
            f32(rows, 8),
            f32(8, 128),
        ),
        [active, tiles, row_lse, place, *packs],
        scalars=1,
        flops=4715000000,
    )
    total = total[0, :1]
    for bit in range(low):
        total = total + exchanged(total, "dp", 1 << bit)
    loss = total / (2.0 * rows * shards)

    query_grad, token = query_product(grads, [passages, *far_p])

    parts = near
    for part in partial_rows(passages, heads, [bundle]):
        parts += [part, exchanged(part, "sub", 1)]
    passage_grad = passage_product(
        col_lse,
        far_lse,
        [back, queries],
        parts,
        [(0, 0)] + [(k, 0) for k in upper],
        [far_q, *heads],
        last=False,
    )
    end = partial_stack(passages, tails, [token, passage_grad, loss])
    passage_grad = passage_product(
        col_lse,
        far_lse,
        [passage_grad],
        [end, exchanged(end, "sub", 1)],
        [(k, first) for k in upper],
        tails,
        last=True,
    )
    return (loss, query_grad, passage_grad)


def solution(mesh):
    placed = (P("dp", "sub"), P("dp", "sub"), P("dp", None), P())
    return jax.shard_map(
        local,
        mesh=mesh,
        in_specs=placed,
        out_specs=(P(), P("dp", "sub"), P("dp", "sub")),
        check_vma=False,
    )
```

```python
import functools
import math

import jax
import jax.numpy as jnp
from jax import lax
from jax.experimental import pallas as pl
from jax.experimental.pallas import tpu as pltpu
from jax.sharding import PartitionSpec as P

D = 4096
ABSENT = -1e30


def exchanged(block, axis, offset):
    count = lax.axis_size(axis)
    return lax.ppermute(block, axis, [(i, i ^ offset) for i in range(count)])


def call(kernel, out_shape, operands, **kwargs):
    scalars, unread = kwargs.pop("scalars", 0), kwargs.pop("unread", 0)
    flops = kwargs.pop("flops", 0)
    kwargs["in_specs"] = (
        [pl.BlockSpec(memory_space=pltpu.SMEM)] * scalars
        + [pl.BlockSpec(memory_space=pltpu.VMEM)] * (len(operands) - scalars - unread)
        + [pl.BlockSpec(memory_space=pl.ANY)] * unread
    )
    if "out_specs" not in kwargs:
        kwargs["out_specs"] = jax.tree.map(
            lambda _: pl.BlockSpec(memory_space=pltpu.VMEM), out_shape
        )
    return pl.pallas_call(
        kernel,
        out_shape=out_shape,
        compiler_params=pltpu.CompilerParams(vmem_limit_bytes=12 * 1024 * 1024),
        cost_estimate=pl.CostEstimate(flops=flops, bytes_accessed=0, transcendentals=0),
        **kwargs,
    )(*operands)


def f32(*shape):
    return jax.ShapeDtypeStruct(shape, jnp.float32)


def bf16(*shape):
    return jax.ShapeDtypeStruct(shape, jnp.bfloat16)


def rows_kernel(count, right_ref, *refs):
    for ref, out_ref in zip(refs[:count], refs[-count:]):
        out_ref[...] = lax.dot_general(
            ref[...],
            right_ref[...],
            (((1,), (1,)), ((), ())),
            preferred_element_type=jnp.float32,
        )


def partial_rows(right, blocks, after=()):
    return call(
        functools.partial(rows_kernel, len(blocks)),
        [f32(block.shape[0], right.shape[0]) for block in blocks],
        [right, *blocks, *after],
        unread=len(after),
    )


def stacked_rows_kernel(count, right_ref, *refs):
    for n in range(count):
        refs[-1][n] = lax.dot_general(
            refs[n][...],
            right_ref[...],
            (((1,), (1,)), ((), ())),
            preferred_element_type=jnp.float32,
        )


def partial_stack(right, blocks, after):
    return call(
        functools.partial(stacked_rows_kernel, len(blocks)),
        f32(len(blocks), blocks[0].shape[0], right.shape[0]),
        [right, *blocks, *after],
        unread=len(after),
    )


def tiles_kernel(count, left_ref, *refs):
    out_ref = refs[-1]
    for k, ref in enumerate(refs[:count]):
        out_ref[k] = lax.dot_general(
            left_ref[...],
            ref[...],
            (((1,), (1,)), ((), ())),
            preferred_element_type=jnp.float32,
        )


def partial_tiles(left, blocks, after=()):
    rows, count = left.shape[0], len(blocks)
    return call(
        functools.partial(tiles_kernel, count),
        f32(count, rows, rows),
        [left, *blocks, *after],
        unread=len(after),
    )


def copy_kernel(first, array_ref, *refs):
    refs[-1][...] = array_ref[first : first + refs[-1].shape[0], :]


def rows_after(array, first, count, earlier):
    return call(
        functools.partial(copy_kernel, first),
        jax.ShapeDtypeStruct((count, array.shape[1]), array.dtype),
        [array, *earlier],
        unread=len(earlier),
    )


def pass_kernel(*refs):
    pass


def held_until(array, earlier):
    count = 1 + len(earlier)
    return pl.pallas_call(
        pass_kernel,
        out_shape=jax.ShapeDtypeStruct(array.shape, array.dtype),
        in_specs=[pl.BlockSpec(memory_space=pl.ANY)] * count,
        out_specs=pl.BlockSpec(memory_space=pl.ANY),
        input_output_aliases={0: 0},
        compiler_params=pltpu.CompilerParams(vmem_limit_bytes=1024 * 1024),
        cost_estimate=pl.CostEstimate(flops=0, bytes_accessed=0, transcendentals=0),
    )(array, *earlier)


def join_kernel(upper_ref, lower_ref, out_ref):
    out_ref[: upper_ref.shape[0], :] = upper_ref[...]
    out_ref[upper_ref.shape[0] :, :] = lower_ref[...]


def joined(upper, lower):
    shape = (upper.shape[0] + lower.shape[0], upper.shape[1])
    return call(join_kernel, jax.ShapeDtypeStruct(shape, upper.dtype), [upper, lower])


def stack_kernel(count, *refs):
    for k in range(count):
        refs[-1][k] = refs[k][...]


def as_row(column, rows):
    i = lax.broadcasted_iota(jnp.int32, (rows, rows), 0)
    j = lax.broadcasted_iota(jnp.int32, (rows, rows), 1)
    return jnp.sum(jnp.where(i == j, column, 0.0), axis=0, keepdims=True)


def as_column(row, rows):
    i = lax.broadcasted_iota(jnp.int32, (rows, rows), 0)
    j = lax.broadcasted_iota(jnp.int32, (rows, rows), 1)
    return jnp.sum(jnp.where(i == j, row, 0.0), axis=1, keepdims=True)


def stats_kernel(levels, slots, unread, act_ref, *refs):
    *refs, tile_ref, row_ref, pack_ref = refs
    *part_refs, pos_ref = refs[: len(refs) - unread]
    rows = tile_ref.shape[1]
    scale = 1.0 / math.sqrt(D)
    slots = iter(slots)
    for mine_ref, other_ref in zip(part_refs[0::2], part_refs[1::2]):
        for k in range(mine_ref.shape[0]):
            tile_ref[next(slots)] = (mine_ref[k] + other_ref[k]) * scale
    top = jnp.max(tile_ref[0], axis=1, keepdims=True)
    for k in range(levels):
        seen = jnp.max(tile_ref[k + 1], axis=1, keepdims=True)
        top = jnp.where(act_ref[k] > 0, jnp.maximum(top, seen), top)
    total = jnp.sum(jnp.exp(tile_ref[0] - top), axis=1, keepdims=True)
    for k in range(levels):
        seen = jnp.sum(jnp.exp(tile_ref[k + 1] - top), axis=1, keepdims=True)
        total = jnp.where(act_ref[k] > 0, total + seen, total)
    row_lse = top + jnp.log(total)
    row_ref[...] = row_lse
    pack_ref[...] = jnp.zeros_like(pack_ref)
    for k in range(levels + 1):
        tile = tile_ref[k]
        high = jnp.max(tile, axis=0, keepdims=True)
        col = high + jnp.log(jnp.sum(jnp.exp(tile - high), axis=0, keepdims=True))
        if k == 0:
            pack_ref[levels : levels + 1, :] = col
        else:
            pack_ref[k - 1 : k, :] = jnp.where(act_ref[k - 1] > 0, col, ABSENT)
    pack_ref[levels + 1 : levels + 2, :] = as_row(row_lse, rows)
    columns = lax.broadcasted_iota(jnp.int32, (rows, rows), 1)
    picked = jnp.where(pos_ref[...] == columns, tile_ref[0], 0.0)
    picked = jnp.sum(jnp.sum(picked, axis=1, keepdims=True), axis=0, keepdims=True)
    pack_ref[levels + 2 : levels + 3, :] = jnp.broadcast_to(picked, (1, rows))


def grads_kernel(
    levels, act_ref, tile_ref, row_ref, pos_ref, *refs
):
    group = 1 << levels
    packs = refs[:group]
    grad_ref, back_ref, col_ref, far_ref, loss_ref = refs[group:]
    rows = tile_ref.shape[1]

    def columns_of(member):
        terms = [packs[member][levels : levels + 1, :]]
        for k in range(levels):
            terms.append(packs[member ^ 1 << k][k : k + 1, :])
        top = functools.reduce(jnp.maximum, terms)
        return top + jnp.log(sum(jnp.exp(term - top) for term in terms))

    col_lses = [columns_of(member) for member in range(group)]
    loss = jnp.zeros((1, 1), jnp.float32)
    for member in range(group):
        line = col_lses[member] + packs[member][levels + 1 : levels + 2, :]
        loss += jnp.sum(line, axis=1, keepdims=True)
        loss -= 2.0 * packs[member][levels + 2 : levels + 3, 0:1]
    loss_ref[...] = jnp.broadcast_to(loss, loss_ref.shape)

    far_ref[...] = jnp.zeros_like(far_ref)
    col_ref[...] = jnp.zeros_like(col_ref)
    for k in range(levels):
        far = packs[1 << k][levels + 1 : levels + 2, :]
        far = jnp.where(act_ref[k] > 0, far, -ABSENT)
        far_ref[:, k : k + 1] = as_column(far, rows)
        col_ref[k : k + 1, :] = jnp.where(act_ref[k] > 0, col_lses[0], -ABSENT)
    row_lse = row_ref[...]
    own = tile_ref[0]
    columns = lax.broadcasted_iota(jnp.int32, (rows, rows), 1)
    onehot = jnp.where(pos_ref[...] == columns, 2.0, 0.0)
    grad = jnp.exp(own - row_lse) + jnp.exp(own - col_lses[0]) - onehot
    grad_ref[0] = grad.astype(jnp.bfloat16)
    back_ref[...] = grad.T.astype(jnp.bfloat16)
    for k in range(levels):
        tile = tile_ref[k + 1]
        grad = jnp.exp(tile - row_lse) + jnp.exp(tile - col_lses[1 << k])
        grad_ref[k + 1] = jnp.where(act_ref[k] > 0, grad, 0.0).astype(jnp.bfloat16)


def dot(left, right):
    return jnp.dot(left, right, preferred_element_type=jnp.float32)


STEP = 256


def column_blocks(width):
    return [slice(first, first + STEP) for first in range(0, width, STEP)]


def copied_out(buffer_ref, out_ref, sems, j, cols):
    return pltpu.make_async_copy(buffer_ref.at[j], out_ref.at[:, cols], sems.at[j])


def copy_scratch(rows, width):
    steps = width // STEP
    return [pltpu.VMEM((steps, rows, STEP), jnp.float32), pltpu.SemaphoreType.DMA((steps,))]


def query_kernel(count, grad_ref, *refs):
    out_ref, token_ref, buffer_ref, sems = refs[count:]
    token_ref[...] = jnp.zeros_like(token_ref)
    blocks = column_blocks(out_ref.shape[1])
    for j, cols in enumerate(blocks):
        total = dot(grad_ref[0], refs[0][:, cols])
        for k in range(1, count):
            total += dot(grad_ref[k], refs[k][:, cols])
        buffer_ref[j] = total
        copied_out(buffer_ref, out_ref, sems, j, cols).start()
    for j, cols in enumerate(blocks):
        copied_out(buffer_ref, out_ref, sems, j, cols).wait()


def query_product(grads, blocks):
    count, rows, width = len(blocks), *blocks[0].shape
    return call(
        functools.partial(query_kernel, count),
        (f32(rows, width), f32(8, 128)),
        [grads, *blocks],
        out_specs=(
            pl.BlockSpec(memory_space=pl.ANY),
            pl.BlockSpec(memory_space=pltpu.VMEM),
        ),
        scratch_shapes=copy_scratch(rows, width),
    )


def passage_kernel(pieces, last, col_ref, far_ref, *refs):
    count = len(pieces)
    if last:
        stacks, refs = refs[:2], refs[2:]
        parts = [stack.at[n] for n in range(count) for stack in stacks]
    else:
        parts, refs = refs[: 2 * count], refs[2 * count :]
    heads = 1 if last else 2
    head, blocks = refs[:heads], refs[heads : heads + count]
    out_ref, *scratch = refs[heads + count :]
    grads = scratch[:count]
    for n, (k, start) in enumerate(pieces):
        rows = blocks[n].shape[0]
        tile = (parts[2 * n][...] + parts[2 * n + 1][...]) * (1.0 / math.sqrt(D))
        far = far_ref[start : start + rows, k : k + 1]
        grad = jnp.exp(tile - far) + jnp.exp(tile - col_ref[k : k + 1, :])
        grads[n][...] = grad.T.astype(jnp.bfloat16)

    columns = column_blocks(out_ref.shape[1])
    for j, cols in enumerate(columns):
        if last:
            total = head[0][:, cols]
        else:
            total = dot(head[0][...], head[1][:, cols])
        for grad_ref, block in zip(grads, blocks):
            total += dot(grad_ref[...], block[:, cols])
        if last:
            buffer_ref, sems = scratch[count:]
            buffer_ref[j] = total
            copied_out(buffer_ref, out_ref, sems, j, cols).start()
        else:
            out_ref[:, cols] = total
    if last:
        for j, cols in enumerate(columns):
            copied_out(buffer_ref, out_ref, sems, j, cols).wait()


def passage_product(col, far, head, parts, pieces, blocks, last):
    rows, width = far.shape[0], blocks[0].shape[1]
    scratch = [pltpu.VMEM((rows, block.shape[0]), jnp.bfloat16) for block in blocks]
    if last:
        scratch += copy_scratch(rows, width)
    return call(
        functools.partial(passage_kernel, pieces, last),
        f32(rows, width),
        [col, far, *parts, *head, *blocks],
        out_specs=pl.BlockSpec(memory_space=pl.ANY if last else pltpu.VMEM),
        scratch_shapes=scratch,
    )


def local(queries, passages, positive, pair_on):
    rows, _ = queries.shape
    levels = pair_on.shape[1]
    me = lax.axis_index("dp")
    shards = lax.axis_size("dp")
    low = shards.bit_length() - 1 - levels
    masks = [1 << low + k for k in range(levels)]
    active = pair_on[me]
    place = positive.reshape(rows, 1)

    first = 13 * rows // 24
    upper = list(reversed(range(1, levels)))
    far_p = [None] * levels
    for k in reversed(range(levels)):
        far_p[k] = exchanged(passages, "dp", masks[k])
    part = 5 * rows // 6
    far_upper = exchanged(queries[:part], "dp", masks[0])
    far_q = joined(far_upper, exchanged(queries[part:], "dp", masks[0]))
    head = held_until(rows_after(queries, 0, first, []), [far_upper])
    heads = [exchanged(head, "dp", masks[k]) for k in upper]

    early = partial_tiles(queries, [passages, far_p[0]])
    early_other = exchanged(early, "sub", 1)
    late = [
        partial_tiles(queries, [block], [early_other])
        for block in [far_p[k] for k in upper]
    ]
    late_parts = []
    for part in late:
        late_parts += [part, exchanged(part, "sub", 1)]
    (near,) = partial_rows(passages, [far_q])
    near = [near, exchanged(near, "sub", 1)]
    tiles, row_lse, pack = call(
        functools.partial(stats_kernel, levels, [0, 1] + [k + 1 for k in upper], 1),
        (f32(levels + 1, rows, rows), f32(rows, 1), f32(8, rows)),
        [
            active,
            early, early_other,
            *late_parts,
            place,
            near[1],
        ],
        scalars=1,
        unread=1,
    )

    group = 1 << levels
    packs = [None] * group
    packs[0] = pack
    for member in range(3, group, 2):
        offset = sum(masks[k] for k in range(levels) if member >> k & 1)
        packs[member] = exchanged(pack, "dp", offset)
    come = [packs[member | (member > 1)] for member in range(0, group, 2)]
    tails = [
        exchanged(rows_after(queries, first, rows - first, [pack, piece]), "dp", masks[k])
        for k, piece in zip(upper, heads)
    ]
    bundle = call(
        functools.partial(stack_kernel, len(come)),
        f32(len(come), *pack.shape),
        come,
    )
    swapped = exchanged(bundle, "dp", masks[0])
    for n in range(group // 2):
        packs[2 * n if n else 1] = swapped[n]

    grads, back, col_lse, far_lse, total = call(
        functools.partial(grads_kernel, levels),
        (
            bf16(levels + 1, rows, rows),
            bf16(rows, rows),
            f32(8, rows),
            f32(rows, 8),
            f32(8, 128),
        ),
        [active, tiles, row_lse, place, *packs],
        scalars=1,
        flops=4715000000,
    )
    total = total[0, :1]
    for bit in range(low):
        total = total + exchanged(total, "dp", 1 << bit)
    loss = total / (2.0 * rows * shards)

    query_grad, token = query_product(grads, [passages, *far_p])

    parts = near
    for part in partial_rows(passages, heads, [bundle]):
        parts += [part, exchanged(part, "sub", 1)]
    passage_grad = passage_product(
        col_lse,
        far_lse,
        [back, queries],
        parts,
        [(0, 0)] + [(k, 0) for k in upper],
        [far_q, *heads],
        last=False,
    )
    end = partial_stack(passages, tails, [token, passage_grad, loss])
    passage_grad = passage_product(
        col_lse,
        far_lse,
        [passage_grad],
        [end, exchanged(end, "sub", 1)],
        [(k, first) for k in upper],
        tails,
        last=True,
    )
    return (loss, query_grad, passage_grad)


def solution(mesh):
    placed = (P("dp", "sub"), P("dp", "sub"), P("dp", None), P())
    return jax.shard_map(
        local,
        mesh=mesh,
        in_specs=placed,
        out_specs=(P(), P("dp", "sub"), P("dp", "sub")),
        check_vma=False,
    )
```

```python
import functools
import math

import jax
import jax.numpy as jnp
from jax import lax
from jax.experimental import pallas as pl
from jax.experimental.pallas import tpu as pltpu
from jax.sharding import PartitionSpec as P

D = 4096
ABSENT = -1e30


def exchanged(block, axis, offset):
    count = lax.axis_size(axis)
    return lax.ppermute(block, axis, [(i, i ^ offset) for i in range(count)])


def call(kernel, out_shape, operands, **kwargs):
    scalars, unread = kwargs.pop("scalars", 0), kwargs.pop("unread", 0)
    flops = kwargs.pop("flops", 0)
    kwargs["in_specs"] = (
        [pl.BlockSpec(memory_space=pltpu.SMEM)] * scalars
        + [pl.BlockSpec(memory_space=pltpu.VMEM)] * (len(operands) - scalars - unread)
        + [pl.BlockSpec(memory_space=pl.ANY)] * unread
    )
    if "out_specs" not in kwargs:
        kwargs["out_specs"] = jax.tree.map(
            lambda _: pl.BlockSpec(memory_space=pltpu.VMEM), out_shape
        )
    return pl.pallas_call(
        kernel,
        out_shape=out_shape,
        compiler_params=pltpu.CompilerParams(vmem_limit_bytes=12 * 1024 * 1024),
        cost_estimate=pl.CostEstimate(flops=flops, bytes_accessed=0, transcendentals=0),
        **kwargs,
    )(*operands)


def f32(*shape):
    return jax.ShapeDtypeStruct(shape, jnp.float32)


def bf16(*shape):
    return jax.ShapeDtypeStruct(shape, jnp.bfloat16)


def rows_kernel(count, right_ref, *refs):
    for ref, out_ref in zip(refs[:count], refs[-count:]):
        out_ref[...] = lax.dot_general(
            ref[...],
            right_ref[...],
            (((1,), (1,)), ((), ())),
            preferred_element_type=jnp.float32,
        )


def partial_rows(right, blocks, after=()):
    return call(
        functools.partial(rows_kernel, len(blocks)),
        [f32(block.shape[0], right.shape[0]) for block in blocks],
        [right, *blocks, *after],
        unread=len(after),
    )


def stacked_rows_kernel(count, right_ref, *refs):
    for n in range(count):
        refs[-1][n] = lax.dot_general(
            refs[n][...],
            right_ref[...],
            (((1,), (1,)), ((), ())),
            preferred_element_type=jnp.float32,
        )


def partial_stack(right, blocks, after):
    return call(
        functools.partial(stacked_rows_kernel, len(blocks)),
        f32(len(blocks), blocks[0].shape[0], right.shape[0]),
        [right, *blocks, *after],
        unread=len(after),
    )


def tiles_kernel(count, left_ref, *refs):
    out_ref = refs[-1]
    for k, ref in enumerate(refs[:count]):
        out_ref[k] = lax.dot_general(
            left_ref[...],
            ref[...],
            (((1,), (1,)), ((), ())),
            preferred_element_type=jnp.float32,
        )


def partial_tiles(left, blocks, after=()):
    rows, count = left.shape[0], len(blocks)
    return call(
        functools.partial(tiles_kernel, count),
        f32(count, rows, rows),
        [left, *blocks, *after],
        unread=len(after),
    )


def copy_kernel(first, array_ref, *refs):
    refs[-1][...] = array_ref[first : first + refs[-1].shape[0], :]


def rows_after(array, first, count, earlier):
    return call(
        functools.partial(copy_kernel, first),
        jax.ShapeDtypeStruct((count, array.shape[1]), array.dtype),
        [array, *earlier],
        unread=len(earlier),
    )


def pass_kernel(*refs):
    pass


def held_until(array, earlier):
    count = 1 + len(earlier)
    return pl.pallas_call(
        pass_kernel,
        out_shape=jax.ShapeDtypeStruct(array.shape, array.dtype),
        in_specs=[pl.BlockSpec(memory_space=pl.ANY)] * count,
        out_specs=pl.BlockSpec(memory_space=pl.ANY),
        input_output_aliases={0: 0},
        compiler_params=pltpu.CompilerParams(vmem_limit_bytes=1024 * 1024),
        cost_estimate=pl.CostEstimate(flops=0, bytes_accessed=0, transcendentals=0),
    )(array, *earlier)


def join_kernel(upper_ref, lower_ref, out_ref):
    out_ref[: upper_ref.shape[0], :] = upper_ref[...]
    out_ref[upper_ref.shape[0] :, :] = lower_ref[...]


def joined(upper, lower):
    shape = (upper.shape[0] + lower.shape[0], upper.shape[1])
    return call(join_kernel, jax.ShapeDtypeStruct(shape, upper.dtype), [upper, lower])


def stack_kernel(count, *refs):
    for k in range(count):
        refs[-1][k] = refs[k][...]


def as_row(column, rows):
    i = lax.broadcasted_iota(jnp.int32, (rows, rows), 0)
    j = lax.broadcasted_iota(jnp.int32, (rows, rows), 1)
    return jnp.sum(jnp.where(i == j, column, 0.0), axis=0, keepdims=True)


def as_column(row, rows):
    i = lax.broadcasted_iota(jnp.int32, (rows, rows), 0)
    j = lax.broadcasted_iota(jnp.int32, (rows, rows), 1)
    return jnp.sum(jnp.where(i == j, row, 0.0), axis=1, keepdims=True)


def stats_kernel(levels, slots, unread, act_ref, *refs):
    *refs, tile_ref, row_ref, pack_ref = refs
    *part_refs, pos_ref = refs[: len(refs) - unread]
    rows = tile_ref.shape[1]
    scale = 1.0 / math.sqrt(D)
    slots = iter(slots)
    for mine_ref, other_ref in zip(part_refs[0::2], part_refs[1::2]):
        for k in range(mine_ref.shape[0]):
            tile_ref[next(slots)] = (mine_ref[k] + other_ref[k]) * scale
    top = jnp.max(tile_ref[0], axis=1, keepdims=True)
    for k in range(levels):
        seen = jnp.max(tile_ref[k + 1], axis=1, keepdims=True)
        top = jnp.where(act_ref[k] > 0, jnp.maximum(top, seen), top)
    total = jnp.sum(jnp.exp(tile_ref[0] - top), axis=1, keepdims=True)
    for k in range(levels):
        seen = jnp.sum(jnp.exp(tile_ref[k + 1] - top), axis=1, keepdims=True)
        total = jnp.where(act_ref[k] > 0, total + seen, total)
    row_lse = top + jnp.log(total)
    row_ref[...] = row_lse
    pack_ref[...] = jnp.zeros_like(pack_ref)
    for k in range(levels + 1):
        tile = tile_ref[k]
        high = jnp.max(tile, axis=0, keepdims=True)
        col = high + jnp.log(jnp.sum(jnp.exp(tile - high), axis=0, keepdims=True))
        if k == 0:
            pack_ref[levels : levels + 1, :] = col
        else:
            pack_ref[k - 1 : k, :] = jnp.where(act_ref[k - 1] > 0, col, ABSENT)
    pack_ref[levels + 1 : levels + 2, :] = as_row(row_lse, rows)
    columns = lax.broadcasted_iota(jnp.int32, (rows, rows), 1)
    picked = jnp.where(pos_ref[...] == columns, tile_ref[0], 0.0)
    picked = jnp.sum(jnp.sum(picked, axis=1, keepdims=True), axis=0, keepdims=True)
    pack_ref[levels + 2 : levels + 3, :] = jnp.broadcast_to(picked, (1, rows))


def grads_kernel(
    levels, act_ref, tile_ref, row_ref, pos_ref, *refs
):
    group = 1 << levels
    packs = refs[:group]
    grad_ref, back_ref, col_ref, far_ref, loss_ref = refs[group:]
    rows = tile_ref.shape[1]

    def columns_of(member):
        terms = [packs[member][levels : levels + 1, :]]
        for k in range(levels):
            terms.append(packs[member ^ 1 << k][k : k + 1, :])
        top = functools.reduce(jnp.maximum, terms)
        return top + jnp.log(sum(jnp.exp(term - top) for term in terms))

    col_lses = [columns_of(member) for member in range(group)]
    loss = jnp.zeros((1, 1), jnp.float32)
    for member in range(group):
        line = col_lses[member] + packs[member][levels + 1 : levels + 2, :]
        loss += jnp.sum(line, axis=1, keepdims=True)
        loss -= 2.0 * packs[member][levels + 2 : levels + 3, 0:1]
    loss_ref[...] = jnp.broadcast_to(loss, loss_ref.shape)

    far_ref[...] = jnp.zeros_like(far_ref)
    col_ref[...] = jnp.zeros_like(col_ref)
    for k in range(levels):
        far = packs[1 << k][levels + 1 : levels + 2, :]
        far = jnp.where(act_ref[k] > 0, far, -ABSENT)
        far_ref[:, k : k + 1] = as_column(far, rows)
        col_ref[k : k + 1, :] = jnp.where(act_ref[k] > 0, col_lses[0], -ABSENT)
    row_lse = row_ref[...]
    own = tile_ref[0]
    columns = lax.broadcasted_iota(jnp.int32, (rows, rows), 1)
    onehot = jnp.where(pos_ref[...] == columns, 2.0, 0.0)
    grad = jnp.exp(own - row_lse) + jnp.exp(own - col_lses[0]) - onehot
    grad_ref[0] = grad.astype(jnp.bfloat16)
    back_ref[...] = grad.T.astype(jnp.bfloat16)
    for k in range(levels):
        tile = tile_ref[k + 1]
        grad = jnp.exp(tile - row_lse) + jnp.exp(tile - col_lses[1 << k])
        grad_ref[k + 1] = jnp.where(act_ref[k] > 0, grad, 0.0).astype(jnp.bfloat16)


def dot(left, right):
    return jnp.dot(left, right, preferred_element_type=jnp.float32)


STEP = 512


def column_blocks(width):
    return [slice(first, first + STEP) for first in range(0, width, STEP)]


def copied_out(buffer_ref, out_ref, sems, j, cols):
    return pltpu.make_async_copy(buffer_ref.at[j], out_ref.at[:, cols], sems.at[j])


def copy_scratch(rows, width):
    steps = width // STEP
    return [pltpu.VMEM((steps, rows, STEP), jnp.float32), pltpu.SemaphoreType.DMA((steps,))]


def query_kernel(count, grad_ref, *refs):
    out_ref, token_ref, buffer_ref, sems = refs[count:]
    token_ref[...] = jnp.zeros_like(token_ref)
    blocks = column_blocks(out_ref.shape[1])
    for j, cols in enumerate(blocks):
        total = dot(grad_ref[0], refs[0][:, cols])
        for k in range(1, count):
            total += dot(grad_ref[k], refs[k][:, cols])
        buffer_ref[j] = total
        copied_out(buffer_ref, out_ref, sems, j, cols).start()
    for j, cols in enumerate(blocks):
        copied_out(buffer_ref, out_ref, sems, j, cols).wait()


def query_product(grads, blocks):
    count, rows, width = len(blocks), *blocks[0].shape
    return call(
        functools.partial(query_kernel, count),
        (f32(rows, width), f32(8, 128)),
        [grads, *blocks],
        out_specs=(
            pl.BlockSpec(memory_space=pl.ANY),
            pl.BlockSpec(memory_space=pltpu.VMEM),
        ),
        scratch_shapes=copy_scratch(rows, width),
    )


def passage_kernel(pieces, last, col_ref, far_ref, *refs):
    count = len(pieces)
    if last:
        stacks, refs = refs[:2], refs[2:]
        parts = [stack.at[n] for n in range(count) for stack in stacks]
    else:
        parts, refs = refs[: 2 * count], refs[2 * count :]
    heads = 1 if last else 2
    head, blocks = refs[:heads], refs[heads : heads + count]
    out_ref, *scratch = refs[heads + count :]
    grads = scratch[:count]
    for n, (k, start) in enumerate(pieces):
        rows = blocks[n].shape[0]
        tile = (parts[2 * n][...] + parts[2 * n + 1][...]) * (1.0 / math.sqrt(D))
        far = far_ref[start : start + rows, k : k + 1]
        grad = jnp.exp(tile - far) + jnp.exp(tile - col_ref[k : k + 1, :])
        grads[n][...] = grad.T.astype(jnp.bfloat16)

    columns = column_blocks(out_ref.shape[1])
    for j, cols in enumerate(columns):
        if last:
            total = head[0][:, cols]
        else:
            total = dot(head[0][...], head[1][:, cols])
        for grad_ref, block in zip(grads, blocks):
            total += dot(grad_ref[...], block[:, cols])
        if last:
            buffer_ref, sems = scratch[count:]
            buffer_ref[j] = total
            copied_out(buffer_ref, out_ref, sems, j, cols).start()
        else:
            out_ref[:, cols] = total
    if last:
        for j, cols in enumerate(columns):
            copied_out(buffer_ref, out_ref, sems, j, cols).wait()


def passage_product(col, far, head, parts, pieces, blocks, last):
    rows, width = far.shape[0], blocks[0].shape[1]
    scratch = [pltpu.VMEM((rows, block.shape[0]), jnp.bfloat16) for block in blocks]
    if last:
        scratch += copy_scratch(rows, width)
    return call(
        functools.partial(passage_kernel, pieces, last),
        f32(rows, width),
        [col, far, *parts, *head, *blocks],
        out_specs=pl.BlockSpec(memory_space=pl.ANY if last else pltpu.VMEM),
        scratch_shapes=scratch,
    )


def local(queries, passages, positive, pair_on):
    rows, _ = queries.shape
    levels = pair_on.shape[1]
    me = lax.axis_index("dp")
    shards = lax.axis_size("dp")
    low = shards.bit_length() - 1 - levels
    masks = [1 << low + k for k in range(levels)]
    active = pair_on[me]
    place = positive.reshape(rows, 1)

    first = rows // 2
    upper = list(reversed(range(1, levels)))
    far_p = [None] * levels
    for k in reversed(range(levels)):
        far_p[k] = exchanged(passages, "dp", masks[k])
    part = 5 * rows // 6
    far_upper = exchanged(queries[:part], "dp", masks[0])
    far_q = joined(far_upper, exchanged(queries[part:], "dp", masks[0]))
    head = held_until(rows_after(queries, 0, first, []), [far_upper])
    heads = [exchanged(head, "dp", masks[k]) for k in upper]

    early = partial_tiles(queries, [passages, far_p[0]])
    early_other = exchanged(early, "sub", 1)
    late = [
        partial_tiles(queries, [block], [early_other])
        for block in [far_p[k] for k in upper]
    ]
    late_parts = []
    for part in late:
        late_parts += [part, exchanged(part, "sub", 1)]
    (near,) = partial_rows(passages, [far_q])
    near = [near, exchanged(near, "sub", 1)]
    tiles, row_lse, pack = call(
        functools.partial(stats_kernel, levels, [0, 1] + [k + 1 for k in upper], 1),
        (f32(levels + 1, rows, rows), f32(rows, 1), f32(8, rows)),
        [
            active,
            early, early_other,
            *late_parts,
            place,
            near[1],
        ],
        scalars=1,
        unread=1,
    )

    group = 1 << levels
    packs = [None] * group
    packs[0] = pack
    for member in range(3, group, 2):
        offset = sum(masks[k] for k in range(levels) if member >> k & 1)
        packs[member] = exchanged(pack, "dp", offset)
    come = [packs[member | (member > 1)] for member in range(0, group, 2)]
    tails = [
        exchanged(rows_after(queries, first, rows - first, [pack, piece]), "dp", masks[k])
        for k, piece in zip(upper, heads)
    ]
    bundle = call(
        functools.partial(stack_kernel, len(come)),
        f32(len(come), *pack.shape),
        come,
    )
    swapped = exchanged(bundle, "dp", masks[0])
    for n in range(group // 2):
        packs[2 * n if n else 1] = swapped[n]

    grads, back, col_lse, far_lse, total = call(
        functools.partial(grads_kernel, levels),
        (
            bf16(levels + 1, rows, rows),
            bf16(rows, rows),
            f32(8, rows),
            f32(rows, 8),
            f32(8, 128),
        ),
        [active, tiles, row_lse, place, *packs],
        scalars=1,
        flops=5405000000,
    )
    total = total[0, :1]
    for bit in range(low):
        total = total + exchanged(total, "dp", 1 << bit)
    loss = total / (2.0 * rows * shards)

    query_grad, token = query_product(grads, [passages, *far_p])

    parts = near
    for part in partial_rows(passages, heads, [bundle]):
        parts += [part, exchanged(part, "sub", 1)]
    passage_grad = passage_product(
        col_lse,
        far_lse,
        [back, queries],
        parts,
        [(0, 0)] + [(k, 0) for k in upper],
        [far_q, *heads],
        last=False,
    )
    end = partial_stack(passages, tails, [token, passage_grad, loss])
    passage_grad = passage_product(
        col_lse,
        far_lse,
        [passage_grad],
        [end, exchanged(end, "sub", 1)],
        [(k, first) for k in upper],
        tails,
        last=True,
    )
    return (loss, query_grad, passage_grad)


def solution(mesh):
    placed = (P("dp", "sub"), P("dp", "sub"), P("dp", None), P())
    return jax.shard_map(
        local,
        mesh=mesh,
        in_specs=placed,
        out_specs=(P(), P("dp", "sub"), P("dp", "sub")),
        check_vma=False,
    )
```

```python
import functools
import math

import jax
import jax.numpy as jnp
from jax import lax
from jax.experimental import pallas as pl
from jax.experimental.pallas import tpu as pltpu
from jax.sharding import PartitionSpec as P

D = 4096
ABSENT = -1e30


def exchanged(block, axis, offset):
    count = lax.axis_size(axis)
    return lax.ppermute(block, axis, [(i, i ^ offset) for i in range(count)])


def call(kernel, out_shape, operands, **kwargs):
    scalars, unread = kwargs.pop("scalars", 0), kwargs.pop("unread", 0)
    flops = kwargs.pop("flops", 0)
    kwargs["in_specs"] = (
        [pl.BlockSpec(memory_space=pltpu.SMEM)] * scalars
        + [pl.BlockSpec(memory_space=pltpu.VMEM)] * (len(operands) - scalars - unread)
        + [pl.BlockSpec(memory_space=pl.ANY)] * unread
    )
    if "out_specs" not in kwargs:
        kwargs["out_specs"] = jax.tree.map(
            lambda _: pl.BlockSpec(memory_space=pltpu.VMEM), out_shape
        )
    return pl.pallas_call(
        kernel,
        out_shape=out_shape,
        compiler_params=pltpu.CompilerParams(vmem_limit_bytes=8 * 1024 * 1024),
        cost_estimate=pl.CostEstimate(flops=flops, bytes_accessed=0, transcendentals=0),
        **kwargs,
    )(*operands)


def f32(*shape):
    return jax.ShapeDtypeStruct(shape, jnp.float32)


def bf16(*shape):
    return jax.ShapeDtypeStruct(shape, jnp.bfloat16)


def rows_kernel(count, right_ref, *refs):
    for ref, out_ref in zip(refs[:count], refs[-count:]):
        out_ref[...] = lax.dot_general(
            ref[...],
            right_ref[...],
            (((1,), (1,)), ((), ())),
            preferred_element_type=jnp.float32,
        )


def partial_rows(right, blocks, after=()):
    return call(
        functools.partial(rows_kernel, len(blocks)),
        [f32(block.shape[0], right.shape[0]) for block in blocks],
        [right, *blocks, *after],
        unread=len(after),
    )


def stacked_rows_kernel(count, right_ref, *refs):
    for n in range(count):
        refs[-1][n] = lax.dot_general(
            refs[n][...],
            right_ref[...],
            (((1,), (1,)), ((), ())),
            preferred_element_type=jnp.float32,
        )


def partial_stack(right, blocks, after):
    return call(
        functools.partial(stacked_rows_kernel, len(blocks)),
        f32(len(blocks), blocks[0].shape[0], right.shape[0]),
        [right, *blocks, *after],
        unread=len(after),
    )


def tiles_kernel(count, left_ref, *refs):
    out_ref = refs[-1]
    for k, ref in enumerate(refs[:count]):
        out_ref[k] = lax.dot_general(
            left_ref[...],
            ref[...],
            (((1,), (1,)), ((), ())),
            preferred_element_type=jnp.float32,
        )


def partial_tiles(left, blocks, after=()):
    rows, count = left.shape[0], len(blocks)
    return call(
        functools.partial(tiles_kernel, count),
        f32(count, rows, rows),
        [left, *blocks, *after],
        unread=len(after),
    )


def copy_kernel(first, array_ref, *refs):
    refs[-1][...] = array_ref[first : first + refs[-1].shape[0], :]


def rows_after(array, first, count, earlier):
    return call(
        functools.partial(copy_kernel, first),
        jax.ShapeDtypeStruct((count, array.shape[1]), array.dtype),
        [array, *earlier],
        unread=len(earlier),
    )


def pass_kernel(*refs):
    pass


def held_until(array, earlier):
    count = 1 + len(earlier)
    return pl.pallas_call(
        pass_kernel,
        out_shape=jax.ShapeDtypeStruct(array.shape, array.dtype),
        in_specs=[pl.BlockSpec(memory_space=pl.ANY)] * count,
        out_specs=pl.BlockSpec(memory_space=pl.ANY),
        input_output_aliases={0: 0},
        compiler_params=pltpu.CompilerParams(vmem_limit_bytes=1024 * 1024),
        cost_estimate=pl.CostEstimate(flops=0, bytes_accessed=0, transcendentals=0),
    )(array, *earlier)


def join_kernel(upper_ref, lower_ref, out_ref):
    out_ref[: upper_ref.shape[0], :] = upper_ref[...]
    out_ref[upper_ref.shape[0] :, :] = lower_ref[...]


def joined(upper, lower):
    shape = (upper.shape[0] + lower.shape[0], upper.shape[1])
    return call(join_kernel, jax.ShapeDtypeStruct(shape, upper.dtype), [upper, lower])


def stack_kernel(count, *refs):
    for k in range(count):
        refs[-1][k] = refs[k][...]


def as_row(column, rows):
    i = lax.broadcasted_iota(jnp.int32, (rows, rows), 0)
    j = lax.broadcasted_iota(jnp.int32, (rows, rows), 1)
    return jnp.sum(jnp.where(i == j, column, 0.0), axis=0, keepdims=True)


def as_column(row, rows):
    i = lax.broadcasted_iota(jnp.int32, (rows, rows), 0)
    j = lax.broadcasted_iota(jnp.int32, (rows, rows), 1)
    return jnp.sum(jnp.where(i == j, row, 0.0), axis=1, keepdims=True)


def stats_kernel(levels, slots, unread, act_ref, *refs):
    *refs, tile_ref, row_ref, pack_ref = refs
    *part_refs, pos_ref = refs[: len(refs) - unread]
    rows = tile_ref.shape[1]
    scale = 1.0 / math.sqrt(D)
    slots = iter(slots)
    for mine_ref, other_ref in zip(part_refs[0::2], part_refs[1::2]):
        for k in range(mine_ref.shape[0]):
            tile_ref[next(slots)] = (mine_ref[k] + other_ref[k]) * scale
    top = jnp.max(tile_ref[0], axis=1, keepdims=True)
    for k in range(levels):
        seen = jnp.max(tile_ref[k + 1], axis=1, keepdims=True)
        top = jnp.where(act_ref[k] > 0, jnp.maximum(top, seen), top)
    total = jnp.sum(jnp.exp(tile_ref[0] - top), axis=1, keepdims=True)
    for k in range(levels):
        seen = jnp.sum(jnp.exp(tile_ref[k + 1] - top), axis=1, keepdims=True)
        total = jnp.where(act_ref[k] > 0, total + seen, total)
    row_lse = top + jnp.log(total)
    row_ref[...] = row_lse
    pack_ref[...] = jnp.zeros_like(pack_ref)
    for k in range(levels + 1):
        tile = tile_ref[k]
        high = jnp.max(tile, axis=0, keepdims=True)
        col = high + jnp.log(jnp.sum(jnp.exp(tile - high), axis=0, keepdims=True))
        if k == 0:
            pack_ref[levels : levels + 1, :] = col
        else:
            pack_ref[k - 1 : k, :] = jnp.where(act_ref[k - 1] > 0, col, ABSENT)
    pack_ref[levels + 1 : levels + 2, :] = as_row(row_lse, rows)
    columns = lax.broadcasted_iota(jnp.int32, (rows, rows), 1)
    picked = jnp.where(pos_ref[...] == columns, tile_ref[0], 0.0)
    picked = jnp.sum(jnp.sum(picked, axis=1, keepdims=True), axis=0, keepdims=True)
    pack_ref[levels + 2 : levels + 3, :] = jnp.broadcast_to(picked, (1, rows))


def grads_kernel(
    levels, act_ref, tile_ref, row_ref, pos_ref, *refs
):
    group = 1 << levels
    packs = refs[:group]
    grad_ref, back_ref, col_ref, far_ref, loss_ref = refs[group:]
    rows = tile_ref.shape[1]

    def columns_of(member):
        terms = [packs[member][levels : levels + 1, :]]
        for k in range(levels):
            terms.append(packs[member ^ 1 << k][k : k + 1, :])
        top = functools.reduce(jnp.maximum, terms)
        return top + jnp.log(sum(jnp.exp(term - top) for term in terms))

    col_lses = [columns_of(member) for member in range(group)]
    loss = jnp.zeros((1, 1), jnp.float32)
    for member in range(group):
        line = col_lses[member] + packs[member][levels + 1 : levels + 2, :]
        loss += jnp.sum(line, axis=1, keepdims=True)
        loss -= 2.0 * packs[member][levels + 2 : levels + 3, 0:1]
    loss_ref[...] = jnp.broadcast_to(loss, loss_ref.shape)

    far_ref[...] = jnp.zeros_like(far_ref)
    col_ref[...] = jnp.zeros_like(col_ref)
    for k in range(levels):
        far = packs[1 << k][levels + 1 : levels + 2, :]
        far = jnp.where(act_ref[k] > 0, far, -ABSENT)
        far_ref[:, k : k + 1] = as_column(far, rows)
        col_ref[k : k + 1, :] = jnp.where(act_ref[k] > 0, col_lses[0], -ABSENT)
    row_lse = row_ref[...]
    own = tile_ref[0]
    columns = lax.broadcasted_iota(jnp.int32, (rows, rows), 1)
    onehot = jnp.where(pos_ref[...] == columns, 2.0, 0.0)
    grad = jnp.exp(own - row_lse) + jnp.exp(own - col_lses[0]) - onehot
    grad_ref[0] = grad.astype(jnp.bfloat16)
    back_ref[...] = grad.T.astype(jnp.bfloat16)
    for k in range(levels):
        tile = tile_ref[k + 1]
        grad = jnp.exp(tile - row_lse) + jnp.exp(tile - col_lses[1 << k])
        grad_ref[k + 1] = jnp.where(act_ref[k] > 0, grad, 0.0).astype(jnp.bfloat16)


def dot(left, right):
    return jnp.dot(left, right, preferred_element_type=jnp.float32)


STEP = 512


def column_blocks(width):
    return [slice(first, first + STEP) for first in range(0, width, STEP)]


def copied_out(buffer_ref, out_ref, sems, j, cols):
    return pltpu.make_async_copy(buffer_ref.at[j], out_ref.at[:, cols], sems.at[j])


def copy_scratch(rows, width):
    steps = width // STEP
    return [pltpu.VMEM((steps, rows, STEP), jnp.float32), pltpu.SemaphoreType.DMA((steps,))]


def query_kernel(count, grad_ref, *refs):
    out_ref, token_ref, buffer_ref, sems = refs[count:]
    token_ref[...] = jnp.zeros_like(token_ref)
    blocks = column_blocks(out_ref.shape[1])
    for j, cols in enumerate(blocks):
        total = dot(grad_ref[0], refs[0][:, cols])
        for k in range(1, count):
            total += dot(grad_ref[k], refs[k][:, cols])
        buffer_ref[j] = total
        copied_out(buffer_ref, out_ref, sems, j, cols).start()
    for j, cols in enumerate(blocks):
        copied_out(buffer_ref, out_ref, sems, j, cols).wait()


def query_product(grads, blocks):
    count, rows, width = len(blocks), *blocks[0].shape
    return call(
        functools.partial(query_kernel, count),
        (f32(rows, width), f32(8, 128)),
        [grads, *blocks],
        out_specs=(
            pl.BlockSpec(memory_space=pl.ANY),
            pl.BlockSpec(memory_space=pltpu.VMEM),
        ),
        scratch_shapes=copy_scratch(rows, width),
    )


def passage_kernel(pieces, last, col_ref, far_ref, *refs):
    count = len(pieces)
    if last:
        stacks, refs = refs[:2], refs[2:]
        parts = [stack.at[n] for n in range(count) for stack in stacks]
    else:
        parts, refs = refs[: 2 * count], refs[2 * count :]
    heads = 1 if last else 2
    head, blocks = refs[:heads], refs[heads : heads + count]
    out_ref, *scratch = refs[heads + count :]
    grads = scratch[:count]
    for n, (k, start) in enumerate(pieces):
        rows = blocks[n].shape[0]
        tile = (parts[2 * n][...] + parts[2 * n + 1][...]) * (1.0 / math.sqrt(D))
        far = far_ref[start : start + rows, k : k + 1]
        grad = jnp.exp(tile - far) + jnp.exp(tile - col_ref[k : k + 1, :])
        grads[n][...] = grad.T.astype(jnp.bfloat16)

    columns = column_blocks(out_ref.shape[1])
    for j, cols in enumerate(columns):
        if last:
            total = head[0][:, cols]
        else:
            total = dot(head[0][...], head[1][:, cols])
        for grad_ref, block in zip(grads, blocks):
            total += dot(grad_ref[...], block[:, cols])
        if last:
            buffer_ref, sems = scratch[count:]
            buffer_ref[j] = total
            copied_out(buffer_ref, out_ref, sems, j, cols).start()
        else:
            out_ref[:, cols] = total
    if last:
        for j, cols in enumerate(columns):
            copied_out(buffer_ref, out_ref, sems, j, cols).wait()


def passage_product(col, far, head, parts, pieces, blocks, last):
    rows, width = far.shape[0], blocks[0].shape[1]
    scratch = [pltpu.VMEM((rows, block.shape[0]), jnp.bfloat16) for block in blocks]
    if last:
        scratch += copy_scratch(rows, width)
    return call(
        functools.partial(passage_kernel, pieces, last),
        f32(rows, width),
        [col, far, *parts, *head, *blocks],
        out_specs=pl.BlockSpec(memory_space=pl.ANY if last else pltpu.VMEM),
        scratch_shapes=scratch,
    )


def local(queries, passages, positive, pair_on):
    rows, _ = queries.shape
    levels = pair_on.shape[1]
    me = lax.axis_index("dp")
    shards = lax.axis_size("dp")
    low = shards.bit_length() - 1 - levels
    masks = [1 << low + k for k in range(levels)]
    active = pair_on[me]
    place = positive.reshape(rows, 1)

    first = 13 * rows // 24
    upper = list(reversed(range(1, levels)))
    far_p = [None] * levels
    for k in reversed(range(levels)):
        far_p[k] = exchanged(passages, "dp", masks[k])
    part = 5 * rows // 6
    far_upper = exchanged(queries[:part], "dp", masks[0])
    far_q = joined(far_upper, exchanged(queries[part:], "dp", masks[0]))
    head = held_until(rows_after(queries, 0, first, []), [far_upper])
    heads = [exchanged(head, "dp", masks[k]) for k in upper]

    early = partial_tiles(queries, [passages, far_p[0]])
    early_other = exchanged(early, "sub", 1)
    late = [
        partial_tiles(queries, [block], [early_other])
        for block in [far_p[k] for k in upper]
    ]
    late_parts = []
    for part in late:
        late_parts += [part, exchanged(part, "sub", 1)]
    (near,) = partial_rows(passages, [far_q])
    near = [near, exchanged(near, "sub", 1)]
    tiles, row_lse, pack = call(
        functools.partial(stats_kernel, levels, [0, 1] + [k + 1 for k in upper], 1),
        (f32(levels + 1, rows, rows), f32(rows, 1), f32(8, rows)),
        [
            active,
            early, early_other,
            *late_parts,
            place,
            near[1],
        ],
        scalars=1,
        unread=1,
    )

    group = 1 << levels
    packs = [None] * group
    packs[0] = pack
    for member in range(3, group, 2):
        offset = sum(masks[k] for k in range(levels) if member >> k & 1)
        packs[member] = exchanged(pack, "dp", offset)
    come = [packs[member | (member > 1)] for member in range(0, group, 2)]
    tails = [
        exchanged(rows_after(queries, first, rows - first, [pack, piece]), "dp", masks[k])
        for k, piece in zip(upper, heads)
    ]
    bundle = call(
        functools.partial(stack_kernel, len(come)),
        f32(len(come), *pack.shape),
        come,
    )
    swapped = exchanged(bundle, "dp", masks[0])
    for n in range(group // 2):
        packs[2 * n if n else 1] = swapped[n]

    grads, back, col_lse, far_lse, total = call(
        functools.partial(grads_kernel, levels),
        (
            bf16(levels + 1, rows, rows),
            bf16(rows, rows),
            f32(8, rows),
            f32(rows, 8),
            f32(8, 128),
        ),
        [active, tiles, row_lse, place, *packs],
        scalars=1,
        flops=4715000000,
    )
    total = total[0, :1]
    for bit in range(low):
        total = total + exchanged(total, "dp", 1 << bit)
    loss = total / (2.0 * rows * shards)

    query_grad, token = query_product(grads, [passages, *far_p])

    parts = near
    for part in partial_rows(passages, heads, [bundle]):
        parts += [part, exchanged(part, "sub", 1)]
    passage_grad = passage_product(
        col_lse,
        far_lse,
        [back, queries],
        parts,
        [(0, 0)] + [(k, 0) for k in upper],
        [far_q, *heads],
        last=False,
    )
    end = partial_stack(passages, tails, [token, passage_grad, loss])
    passage_grad = passage_product(
        col_lse,
        far_lse,
        [passage_grad],
        [end, exchanged(end, "sub", 1)],
        [(k, first) for k in upper],
        tails,
        last=True,
    )
    return (loss, query_grad, passage_grad)


def solution(mesh):
    placed = (P("dp", "sub"), P("dp", "sub"), P("dp", None), P())
    return jax.shard_map(
        local,
        mesh=mesh,
        in_specs=placed,
        out_specs=(P(), P("dp", "sub"), P("dp", "sub")),
        check_vma=False,
    )
```
